32 devices in a mesh: st: 4 (over z), tm: 4 (over x, core), pol: 2 (over y).
Axes of the slice: x: 2, y: 2, z: 4, core: 2. Of those that a mesh axis runs over, the one named last changes fastest.
Arguments:
- samples: bfloat16 [512, 262144], P('st', 'tm'), may hold values from -6 to 6
- history: bfloat16 [512, 24576], P('st'), may hold values from -6 to 6
- station_order: int32 [256], replicated, may hold values from 0 to 255, each once
- channel_order: int32 [2048], replicated, may hold values from 0 to 2047, each once
- flagged: int32 [256], replicated, may hold values 0 or 1
Outputs:
- packed: float32 [2048, 512, 512], P(('st', 'tm', 'pol'))
The draws below stay inside these ranges and needn't reach their ends.
Inputs may be any that keep to these rules, and one draw needn't show every extreme that they name: `station_order`: each station number appears once. `channel_order`: each channel appears once.
All inputs are finite; a program needn't handle non-finite values.
Results may differ from the reference program's by a relative error of at most 0.0082.
Values may be sent and summed in bfloat16 or wider, within the bound.
No kernel may reach another device: no remote copies, remote signals or barrier semaphores. Data moves between devices by JAX's collectives and lax.ppermute only.
A program may use at most 320 MiB of HBM per device.

```python
import math
import jax
import jax.numpy as jnp
from jax import lax

STATIONS = 256
NFFT = 8192
FRAME_A = 32
CH = 2048
TAPS = 4
INPUTS = 512
SAMPLES = 262144


def plant(array, key, least, top_value):
    place = [jax.random.randint(jax.random.fold_in(key, axis), (), 0, length) for axis, length in enumerate(array.shape)]
    main_axis = array.shape.index(max(array.shape))
    neighbour = place[:main_axis] + [(place[main_axis] + 1) % array.shape[main_axis]] + place[main_axis + 1:]
    return array.at[tuple(place)].set(least).at[tuple(neighbour)].set(top_value)


def levels(key, extent, shards, smallest, largest):
    def one(dim, shards_of):
        draws = jax.random.uniform(jax.random.fold_in(jax.random.fold_in(key, 6), dim), (shards_of,), jnp.float32, smallest / len(shards), largest / len(shards))
        return jnp.repeat(jnp.exp(draws), extent[dim] // shards_of).reshape((-1,) + (1,) * (len(extent) - dim - 1))

    level = one(*shards[0])
    for cut in shards[1:]:
        level = level * one(*cut)
    return level


def scatter_about(own_key, dims, deviation, most, pieces=(), dtype=jnp.bfloat16):
    entries = jax.random.normal(own_key, dims, jnp.float32) * deviation
    if len(pieces) > 0:
        entries = levels(own_key, dims, pieces, -0.22, 0.18) * entries
    return jnp.clip(entries, min=-most, max=most).astype(dtype)


def setup_inputs(seed: int = 0) -> dict:
    splits = jax.random.split(jax.random.key(seed), 6)
    samples = scatter_about(splits[0], (INPUTS, SAMPLES), 1.0, 6.0, ((0, 4), (1, 4)))
    history = scatter_about(splits[1], (INPUTS, (TAPS - 1) * NFFT), 1.0, 6.0, ((0, 4),))
    station_order = jax.random.permutation(splits[2], STATIONS).astype(jnp.int32)
    channel_order = jax.random.permutation(splits[3], CH).astype(jnp.int32)
    flagged = plant((jax.random.randint(splits[4], (STATIONS,), 0, 8) < 1).astype(jnp.int32), jax.random.fold_in(splits[4], 1), 0, 1)
    return dict(samples=samples, history=history, station_order=station_order, channel_order=channel_order, flagged=flagged)


def filter_window(tap_count, frame_size):
    length = tap_count * frame_size
    offsets = jnp.arange(length).astype(jnp.float32) + 0.5
    centred = (offsets - 0.5 * length) / frame_size
    tapering = 0.5 - 0.5 * jnp.cos(offsets * (2.0 * math.pi / length))
    return (jnp.sinc(centred) * tapering).reshape(tap_count, frame_size)

def polyphase(row_block, weights, spec_count):
    row_total = row_block.shape[0]
    tap_count, frame_size = weights.shape
    running = jnp.zeros((row_total, spec_count, frame_size), jnp.float32)
    for tap_index in range(tap_count):
        section = row_block[:, tap_index * frame_size:(tap_index + spec_count) * frame_size]
        section = section.reshape(row_total, spec_count, frame_size)
        running = running + section.astype(jnp.float32) * weights[tap_index]
    return running.astype(jnp.bfloat16).reshape(row_total * spec_count, frame_size)

def trig_pair(left, right, modulus, amplitude):
    turn_count = left.astype(jnp.int32)[:, None] * right.astype(jnp.int32)[None, :] % modulus
    angles = turn_count.astype(jnp.float32) * (2.0 * math.pi / modulus)
    cosine = (jnp.cos(angles) * amplitude).astype(jnp.bfloat16)
    sine_part = (-(jnp.sin(angles) * amplitude)).astype(jnp.bfloat16)
    return (cosine, sine_part)

def product_high(form, left, right):
    return jnp.einsum(form, left.astype(jnp.float32), right.astype(jnp.float32), precision=lax.Precision.HIGHEST)

def frame_transform(filtered, channels, first_len):
    row_total, frame_size = filtered.shape
    second_len = frame_size // first_len
    half_len = second_len // 2
    first_idx = jnp.arange(first_len).astype(jnp.int32)
    second_idx = jnp.arange(second_len).astype(jnp.int32)
    half_idx = jnp.arange(half_len).astype(jnp.int32)
    first_cos, first_sin = trig_pair(first_idx, first_idx, first_len, 1.0 / math.sqrt(first_len))
    blocks = filtered.reshape(row_total, first_len, second_len)
    segment_re = product_high('rab,ae->reb', blocks, first_cos)
    segment_im = product_high('rab,ae->reb', blocks, first_sin)
    twist_turns = first_idx[:, None] * second_idx[None, :] % frame_size
    twist_angles = twist_turns.astype(jnp.float32) * (2.0 * math.pi / frame_size)
    twist_cos = jnp.cos(twist_angles)
    twist_sin = jnp.sin(twist_angles)
    twist_re = (segment_re * twist_cos + segment_im * twist_sin).astype(jnp.bfloat16)
    twist_im = (segment_im * twist_cos - segment_re * twist_sin).astype(jnp.bfloat16)
    second_cos, second_sin = trig_pair(second_idx, half_idx, second_len, 1.0 / math.sqrt(second_len))
    full_re = product_high('reb,bf->ref', twist_re, second_cos) - product_high('reb,bf->ref', twist_im, second_sin)
    full_im = product_high('reb,bf->ref', twist_re, second_sin) + product_high('reb,bf->ref', twist_im, second_cos)
    channels = channels.astype(jnp.int32)
    column = (channels % first_len * half_len + channels // first_len).astype(jnp.int32)
    flat_re = full_re.reshape(row_total, first_len * half_len)[:, column]
    flat_im = full_im.reshape(row_total, first_len * half_len)[:, column]
    return jnp.stack([flat_re, flat_im], axis=1)

def input_rows(station_order):
    station_total = station_order.shape[0]
    inverse = jnp.zeros((station_total,), jnp.int32).at[station_order.astype(jnp.int32)].set(jnp.arange(station_total).astype(jnp.int32))
    polarity = jnp.tile(jnp.arange(2).astype(jnp.int32), station_total)
    return (2 * jnp.repeat(inverse, 2) + polarity).astype(jnp.int32)

def packed_visibility(values, norm_scale):
    input_count, spec_count, pair_count, slot_count = values.shape
    arranged = values.transpose(3, 0, 1, 2)
    stacked = arranged.reshape(slot_count, input_count, spec_count * 2)
    swapped = jnp.stack([-arranged[..., 1], arranged[..., 0]], axis=-1).reshape(slot_count, input_count, spec_count * 2)
    combined = jnp.concatenate([stacked, swapped], axis=1)
    visible = jnp.einsum('sik,sjk->sij', stacked, combined, precision=lax.Precision.HIGHEST)
    indices = jnp.arange(input_count)
    upper_half = indices[:, None] <= indices[None, :]
    return jnp.where(upper_half[None], visible[:, :, :input_count], visible[:, :, input_count:]) * norm_scale

def reference(samples, history, station_order, channel_order, flagged):
    spec_total = samples.shape[1] // NFFT
    weights = filter_window(TAPS, NFFT)
    stream = jnp.concatenate([history, samples], axis=1)
    block_rows = min(16, INPUTS)
    block_count = INPUTS // block_rows
    keeping = (1 - flagged[station_order.astype(jnp.int32)]).astype(jnp.float32)
    keep_rows = jnp.repeat(keeping, 2)
    stream_blocks = stream.reshape(block_count, block_rows, stream.shape[1])
    keep_blocks = keep_rows.reshape(block_count, block_rows)

    def transform(operand):
        row_block, keep_block = operand
        filtered = polyphase(row_block, weights, spec_total)
        product = frame_transform(filtered, channel_order, FRAME_A)
        product = product.reshape(block_rows, spec_total, 2, CH) * keep_block[:, None, None, None]
        return product.astype(jnp.bfloat16)
    spectra = lax.map(transform, (stream_blocks, keep_blocks)).reshape(INPUTS, spec_total, 2, CH)
    ordered = spectra[input_rows(station_order)]
    slot_block = min(16, CH)
    slot_groups = CH // slot_block
    grouped = ordered.reshape(INPUTS, spec_total, 2, slot_groups, slot_block).transpose(3, 0, 1, 2, 4)
    norm_scale = 1.0 / spec_total

    def correlate(group):
        return packed_visibility(group.astype(jnp.float32), norm_scale)
    return lax.map(correlate, grouped).reshape(CH, INPUTS, INPUTS)
```

```python
import functools
import math

import jax
import jax.numpy as jnp
import numpy as np
from jax import lax
from jax.experimental import pallas as pl
from jax.experimental.pallas import tpu as pltpu
from jax.sharding import PartitionSpec as P

NFFT = 8192
FRAME_A = 32
FRAME_B = NFFT // FRAME_A
CH = 2048
TAPS = 4
LEAD = TAPS - 1
HALF_E = FRAME_A // 2
LOW = CH // FRAME_A
AXES = ("st", "tm", "pol")
ROWS = 64
GROUP = 16
BATCH = 4
VMEM = 56 << 20


def np_window():
    length = TAPS * NFFT
    offsets = np.arange(length) + 0.5
    centred = (offsets - 0.5 * length) / NFFT
    tapering = 0.5 - 0.5 * np.cos(offsets * (2.0 * math.pi / length))
    return (np.sinc(centred) * tapering).reshape(TAPS, NFFT).astype(np.float32)


def np_first():
    turns = np.arange(FRAME_A)[:, None] * np.arange(FRAME_A)[None, :] % FRAME_A
    angles = turns * (2.0 * math.pi / FRAME_A)
    cosine = np.cos(angles) / math.sqrt(FRAME_A)
    sine = -np.sin(angles) / math.sqrt(FRAME_A)
    rows = [cosine[0], cosine[HALF_E]]
    for e in range(1, HALF_E):
        rows += [cosine[e], sine[e]]
    return np.kron(np.stack(rows), np.eye(GROUP)).astype(jnp.bfloat16)


def np_twist():
    turns = np.arange(HALF_E + 1)[:, None] * np.arange(FRAME_B)[None, :] % NFFT
    angles = turns * (2.0 * math.pi / NFFT)
    return np.cos(angles).astype(np.float32), np.sin(angles).astype(np.float32)


def np_second():
    f = np.concatenate([np.arange(LOW), FRAME_B - 1 - np.arange(LOW)])
    sign = np.where(np.arange(2 * LOW) < LOW, 1.0, -1.0)[:, None]
    angles = f[:, None] * np.arange(FRAME_B)[None, :] % FRAME_B * (2.0 * math.pi / FRAME_B)
    cosine = np.cos(angles) / math.sqrt(FRAME_B)
    sine = -np.sin(angles) / math.sqrt(FRAME_B)
    top = np.concatenate([cosine, -sine], axis=1)
    bottom = np.concatenate([sine * sign, cosine * sign], axis=1)
    return np.concatenate([top, bottom]).astype(jnp.bfloat16)


def filterbank_body(first, taps_of, sizes, step, refs):
    w_ref, c1_ref, cos_ref, sin_ref, w2_ref, pick_ref, outs, y_ref, t_ref, d_ref = refs

    def filter_a(a, carry):
        weights = [w_ref[k : k + 1, pl.ds(pl.multiple_of(a * FRAME_B, FRAME_B), FRAME_B)] for k in range(TAPS)]
        frames = [taps_of(i, a) for i in range(BATCH + LEAD)]
        for t in range(BATCH):
            total = frames[t] * weights[0]
            for k in range(1, TAPS):
                total = total + frames[t + k] * weights[k]
            y_ref[t, pl.ds(pl.multiple_of(a * GROUP, GROUP), GROUP), :] = total.astype(jnp.bfloat16)
        return carry

    lax.fori_loop(0, FRAME_A, filter_a, 0, unroll=2)

    def first_t(t, carry):
        seg = jnp.dot(c1_ref[...], y_ref[t], preferred_element_type=jnp.float32)
        rows = pl.ds(pl.multiple_of(t * ROWS + step * GROUP, GROUP), GROUP)
        for e in range(HALF_E + 1):
            cosine = cos_ref[e : e + 1, :]
            sine = sin_ref[e : e + 1, :]
            if e == 0 or e == HALF_E:
                at = 0 if e == 0 else GROUP
                re = seg[at : at + GROUP]
                twist_re = re * cosine
                twist_im = -(re * sine)
            else:
                at = 2 * e * GROUP
                re = seg[at : at + GROUP]
                im = seg[at + GROUP : at + 2 * GROUP]
                twist_re = re * cosine + im * sine
                twist_im = im * cosine - re * sine
            t_ref[e, rows, 0:FRAME_B] = twist_re.astype(jnp.bfloat16)
            t_ref[e, rows, FRAME_B : 2 * FRAME_B] = twist_im.astype(jnp.bfloat16)
        return carry

    lax.fori_loop(0, BATCH, first_t, 0)

    @pl.when(step == ROWS // GROUP - 1)
    def _():
        width = BATCH * ROWS

        def second_e(e, carry):
            full = lax.dot_general(
                w2_ref[...], t_ref[e], (((1,), (1,)), ((), ())), preferred_element_type=jnp.float32
            )
            rows = pl.ds(pl.multiple_of(e * 2 * LOW, 2 * LOW), 2 * LOW)
            d_ref[rows, 0:width] = full[: 2 * LOW].astype(jnp.bfloat16)
            d_ref[rows, width : 2 * width] = full[2 * LOW :].astype(jnp.bfloat16)
            return carry

        lax.fori_loop(0, HALF_E + 1, second_e, 0)

        peers, share = sizes
        block = 256
        group = block // share

        def gather(i, carry):
            wanted = pick_ref[pl.ds(pl.multiple_of(i * block, block), block), :]
            lanes = lax.broadcasted_iota(jnp.int32, (block, 128), 1)
            hot = jnp.concatenate(
                [
                    jnp.where(wanted == lanes + 128 * k, 1.0, 0.0).astype(jnp.bfloat16)
                    for k in range(HALF_E + 1)
                ],
                axis=1,
            )
            picked = jnp.dot(hot, d_ref[...], preferred_element_type=jnp.float32).astype(jnp.bfloat16)
            part = share // len(outs)
            for j in range(group):
                for h, out_ref in enumerate(outs):
                    out_ref[i * group + j] = picked[j * share + h * part : j * share + (h + 1) * part]
            return carry

        lax.fori_loop(0, peers * share // block, gather, 0)


def late_kernel(sizes, place_ref, x_ref, w_ref, c1_ref, cos_ref, sin_ref, w2_ref, pick_ref, *rest):
    outs, (y_ref, t_ref, d_ref) = rest[:-3], rest[-3:]
    first = x_ref.shape[1] // NFFT - BATCH

    def taps_of(i, a):
        at = (first - LEAD + i) * NFFT
        return x_ref[:, pl.ds(pl.multiple_of(at + a * FRAME_B, FRAME_B), FRAME_B)].astype(jnp.float32)

    refs = (w_ref, c1_ref, cos_ref, sin_ref, w2_ref, pick_ref, outs, y_ref, t_ref, d_ref)
    filterbank_body(first, taps_of, sizes, pl.program_id(0), refs)


def early_kernel(
    sizes, place_ref, x_ref, halo_ref, history_ref, w_ref, c1_ref, cos_ref, sin_ref, w2_ref, pick_ref, *rest
):
    outs, (y_ref, t_ref, d_ref) = rest[:-3], rest[-3:]
    opening = place_ref[1] == 0

    def taps_of(i, a):
        if i >= LEAD:
            at = pl.multiple_of((i - LEAD) * NFFT + a * FRAME_B, FRAME_B)
            return x_ref[:, pl.ds(at, FRAME_B)].astype(jnp.float32)
        at = pl.multiple_of(i * NFFT + a * FRAME_B, FRAME_B)
        mine = halo_ref[:, pl.ds(at, FRAME_B)].astype(jnp.float32)
        old = history_ref[:, pl.ds(at, FRAME_B)].astype(jnp.float32)
        return jnp.where(opening, old, mine)

    refs = (w_ref, c1_ref, cos_ref, sin_ref, w2_ref, pick_ref, outs, y_ref, t_ref, d_ref)
    filterbank_body(0, taps_of, sizes, pl.program_id(0), refs)


def filterbank(kernel, name, peers, share, parts, place, streams, stream_specs, consts):
    whole = [pl.BlockSpec(c.shape, lambda i, p: (0, 0)) for c in consts]
    out = jax.ShapeDtypeStruct((peers, share // parts, 2 * BATCH * ROWS), jnp.bfloat16)
    return pl.pallas_call(
        functools.partial(kernel, (peers, share)),
        out_shape=[out] * parts,
        grid_spec=pltpu.PrefetchScalarGridSpec(
            num_scalar_prefetch=1,
            grid=(ROWS // GROUP,),
            in_specs=stream_specs + whole,
            out_specs=[pl.BlockSpec(out.shape, lambda i, p: (0, 0, 0))] * parts,
            scratch_shapes=[
                pltpu.VMEM((BATCH, FRAME_A * GROUP, FRAME_B), jnp.bfloat16),
                pltpu.VMEM((HALF_E + 1, BATCH * ROWS, 2 * FRAME_B), jnp.bfloat16),
                pltpu.VMEM(((HALF_E + 1) * 2 * LOW, 2 * BATCH * ROWS), jnp.bfloat16),
            ],
        ),
        cost_estimate=pl.CostEstimate(flops=12 * 10**9, bytes_accessed=16 << 20, transcendentals=0),
        compiler_params=pltpu.CompilerParams(
            dimension_semantics=("arbitrary",), vmem_limit_bytes=VMEM
        ),
        name=name,
    )(place, *streams, *consts)


def correlate_kernel(scale, st_count, tm_count, pol_count, per_step, *refs):
    late_ref, early_ref, perm_ref = refs[:3]
    out_ref, lhs_ref, z_ref = refs[-3:]
    step = pl.program_id(0)
    width = BATCH * ROWS
    inputs = out_ref.shape[1]
    pairs = BATCH // 2
    units = st_count * pol_count

    @pl.when(step % (GROUP // per_step) == 0)
    def _():
        row = 0
        for c in range(2):
            for source in (early_ref, late_ref):
                for tm in range(tm_count):
                    for pair in range(pairs):
                        at = c * width + pair * 128
                        for st in range(st_count):
                            for pol in range(pol_count):
                                unit = st * pol_count + pol
                                lhs_ref[row : row + GROUP, unit * 128 : (unit + 1) * 128] = source[
                                    (st * tm_count + tm) * pol_count + pol, :, at : at + 128
                                ]
                        row += GROUP
        for half in range(2):
            turned = jnp.dot(
                lhs_ref[...],
                perm_ref[:, half * inputs : (half + 1) * inputs],
                preferred_element_type=jnp.float32,
            )
            for j in range(inputs // 128):
                z_ref[half * (inputs // 128) + j] = turned[:, j * 128 : (j + 1) * 128]

    depth = 2 * tm_count * pairs
    mid = inputs // 2
    tall = lax.broadcasted_iota(jnp.int32, (mid, mid), 0)
    wide = lax.broadcasted_iota(jnp.int32, (mid, mid), 1)
    upper = tall <= wide

    def one(i, carry):
        slot = lax.rem(step, GROUP // per_step) * per_step + i

        def rows(half, c):
            tiles = [
                z_ref[
                    half * (inputs // 128) + j,
                    pl.ds(c * depth * GROUP + slot, depth, stride=GROUP),
                    :,
                ]
                for j in range(inputs // 128)
            ]
            return jnp.concatenate(tiles, axis=1)

        re0, im0, re1, im1 = rows(0, 0), rows(0, 1), rows(1, 0), rows(1, 1)
        z = jnp.concatenate([re0, im0, re1, im1], axis=0)
        turned = jnp.concatenate([-im0, re0, -im1, re1], axis=0).astype(jnp.bfloat16)
        left = z.T.astype(jnp.bfloat16)
        z = z.astype(jnp.bfloat16)
        dot = functools.partial(jnp.dot, preferred_element_type=jnp.float32)
        for h in range(2):
            here = slice(h * mid, (h + 1) * mid)
            re = dot(left[here], z[:, here])
            im = dot(left[here], turned[:, here])
            out_ref[i, here, here] = jnp.where(upper, re, im) * scale
        out_ref[i, :mid, mid:] = dot(left[:mid], z[:, mid:]) * scale
        out_ref[i, mid:, :mid] = dot(left[mid:], turned[:, :mid]) * scale
        return carry

    lax.fori_loop(0, per_step, one, 0)


def correlate(half, halves, share, inputs, scale, sizes, late, early, perm, before):
    st_count, tm_count, pol_count = sizes
    per_step = 4
    part = share // halves
    steps = part // per_step
    prep = GROUP // per_step
    peers, _, wide = late.shape
    first_prep = half * (part // GROUP)
    first_step = half * steps
    in_specs = [
        pl.BlockSpec((peers, GROUP, wide), lambda i: (0, first_prep + i // prep, 0)),
        pl.BlockSpec((peers, GROUP, wide), lambda i: (0, i // prep, 0)),
        pl.BlockSpec(perm.shape, lambda i: (0, 0)),
    ]
    operands = [late, early, perm]
    aliases = {}
    if before is not None:
        in_specs.append(pl.BlockSpec(memory_space=pl.ANY))
        operands.append(before)
        aliases = {3: 0}
    return pl.pallas_call(
        functools.partial(correlate_kernel, scale, st_count, tm_count, pol_count, per_step),
        out_shape=jax.ShapeDtypeStruct((share, inputs, inputs), jnp.float32),
        grid=(steps,),
        in_specs=in_specs,
        out_specs=pl.BlockSpec((per_step, inputs, inputs), lambda i: (first_step + i, 0, 0)),
        scratch_shapes=[
            pltpu.VMEM((2 * 2 * tm_count * (BATCH // 2) * GROUP, perm.shape[0]), jnp.bfloat16),
            pltpu.VMEM((2 * inputs // 128, 2 * 2 * tm_count * (BATCH // 2) * GROUP, 128), jnp.float32),
        ],
        input_output_aliases=aliases,
        cost_estimate=pl.CostEstimate(
            flops=part * 12 * 10**7, bytes_accessed=part * inputs * inputs * 4, transcendentals=0
        ),
        compiler_params=pltpu.CompilerParams(
            dimension_semantics=("arbitrary",), vmem_limit_bytes=VMEM
        ),
        name="correlate",
    )(*operands)


def fused_body(samples, history, station_order, channel_order, flagged):
    row_count, local_length = samples.shape
    spec_local = local_length // NFFT
    st_count = lax.axis_size("st")
    tm_count = lax.axis_size("tm")
    pol_count = lax.axis_size("pol")
    peers = st_count * tm_count * pol_count
    share = CH // peers
    inputs = row_count * st_count
    pol = lax.axis_index("pol")
    place = jnp.stack([pol, lax.axis_index("tm")]).astype(jnp.int32)

    tail = lax.dynamic_slice(
        samples, (pol * ROWS, local_length - LEAD * NFFT), (ROWS, LEAD * NFFT)
    )
    halo = lax.ppermute(tail, "tm", [(i, i + 1) for i in range(tm_count - 1)])

    e, f = channel_order % FRAME_A, channel_order // FRAME_A
    row = jnp.minimum(e, FRAME_A - e) * (2 * LOW) + jnp.where(e > HALF_E, LOW, 0) + f
    pick = jnp.broadcast_to(row.astype(jnp.int32)[:, None], (CH, 128))
    cosine, sine = np_twist()
    consts = [
        jnp.asarray(c) for c in (np_window(), np_first(), cosine, sine, np_second())
    ] + [pick]

    groups = ROWS // GROUP
    late = filterbank(
        late_kernel, "filterbank_late", peers, share, 1, place, [samples],
        [pl.BlockSpec((GROUP, local_length), lambda i, p: (p[0] * groups + i, 0))],
        consts,
    )
    late = lax.all_to_all(late[0], AXES, split_axis=0, concat_axis=0, tiled=True)
    early = filterbank(
        early_kernel, "filterbank_early", peers, share, 2, place, [samples, halo, history],
        [
            pl.BlockSpec((GROUP, BATCH * NFFT), lambda i, p: (p[0] * groups + i, 0)),
            pl.BlockSpec((GROUP, LEAD * NFFT), lambda i, p: (i, 0)),
            pl.BlockSpec((GROUP, LEAD * NFFT), lambda i, p: (p[0] * groups + i, 0)),
        ],
        consts,
    )
    early = [lax.all_to_all(x, AXES, split_axis=0, concat_axis=0, tiled=True) for x in early]

    global_row = jnp.arange(inputs)
    target = 2 * jnp.repeat(station_order, 2) + global_row % 2
    keep = 1 - jnp.repeat(flagged, 2)
    hot = (target[:, None] == jnp.arange(inputs)[None, :]) & (keep[None, :] == 1)
    hot = hot.astype(jnp.bfloat16).reshape(st_count * pol_count, 1, ROWS, 1, inputs)
    pair = jnp.eye(2, dtype=jnp.bfloat16).reshape(1, 2, 1, 2, 1)
    perm = (hot * pair).reshape(2 * inputs, 2 * inputs)

    scale = 1.0 / (spec_local * tm_count)
    sizes = (st_count, tm_count, pol_count)
    out = None
    for half in range(2):
        out = correlate(half, 2, share, inputs, scale, sizes, late, early[half], perm, out)
    return out


def shifted(array, axis, by):
    peers = lax.axis_size(axis)
    pairs = [(i, i + by) for i in range(peers) if 0 <= i + by < peers]
    return lax.ppermute(array, axis, pairs)


def filter_window(tap_count, frame_size):
    length = tap_count * frame_size
    offsets = jnp.arange(length).astype(jnp.float32) + 0.5
    centred = (offsets - 0.5 * length) / frame_size
    tapering = 0.5 - 0.5 * jnp.cos(offsets * (2.0 * math.pi / length))
    return (jnp.sinc(centred) * tapering).reshape(tap_count, frame_size)


def polyphase(row_block, weights, spec_count):
    row_total = row_block.shape[0]
    tap_count, frame_size = weights.shape
    running = jnp.zeros((row_total, spec_count, frame_size), jnp.float32)
    for tap_index in range(tap_count):
        section = row_block[:, tap_index * frame_size : (tap_index + spec_count) * frame_size]
        section = section.reshape(row_total, spec_count, frame_size)
        running = running + section.astype(jnp.float32) * weights[tap_index]
    return running.astype(jnp.bfloat16).reshape(row_total * spec_count, frame_size)


def trig_pair(left, right, modulus, amplitude):
    turn_count = left[:, None] * right[None, :] % modulus
    angles = turn_count.astype(jnp.float32) * (2.0 * math.pi / modulus)
    cosine = (jnp.cos(angles) * amplitude).astype(jnp.bfloat16)
    sine_part = (-(jnp.sin(angles) * amplitude)).astype(jnp.bfloat16)
    return (cosine, sine_part)


def product_low(form, left, right):
    return jnp.einsum(form, left, right, preferred_element_type=jnp.float32)


def frame_transform(filtered, channels, first_len):
    row_total, frame_size = filtered.shape
    second_len = frame_size // first_len
    half_len = second_len // 2
    first_idx = jnp.arange(first_len)
    second_idx = jnp.arange(second_len)
    half_idx = jnp.arange(half_len)
    first_cos, first_sin = trig_pair(first_idx, first_idx, first_len, 1.0 / math.sqrt(first_len))
    blocks = filtered.reshape(row_total, first_len, second_len)
    segment_re = product_low("rab,ae->reb", blocks, first_cos)
    segment_im = product_low("rab,ae->reb", blocks, first_sin)
    twist_turns = first_idx[:, None] * second_idx[None, :] % frame_size
    twist_angles = twist_turns.astype(jnp.float32) * (2.0 * math.pi / frame_size)
    twist_cos = jnp.cos(twist_angles)
    twist_sin = jnp.sin(twist_angles)
    twist_re = (segment_re * twist_cos + segment_im * twist_sin).astype(jnp.bfloat16)
    twist_im = (segment_im * twist_cos - segment_re * twist_sin).astype(jnp.bfloat16)
    second_cos, second_sin = trig_pair(
        second_idx, half_idx, second_len, 1.0 / math.sqrt(second_len)
    )
    full_re = product_low("reb,bf->ref", twist_re, second_cos) - product_low(
        "reb,bf->ref", twist_im, second_sin
    )
    full_im = product_low("reb,bf->ref", twist_re, second_sin) + product_low(
        "reb,bf->ref", twist_im, second_cos
    )
    column = channels % first_len * half_len + channels // first_len
    flat_re = jnp.take(full_re.reshape(row_total, first_len * half_len), column, axis=1)
    flat_im = jnp.take(full_im.reshape(row_total, first_len * half_len), column, axis=1)
    return jnp.stack([flat_re, flat_im], axis=1)


def input_rows(station_order):
    station_total = station_order.shape[0]
    inverse = (
        jnp.zeros((station_total,), jnp.int32).at[station_order].set(jnp.arange(station_total))
    )
    polarity = jnp.tile(jnp.arange(2), station_total)
    return 2 * jnp.repeat(inverse, 2) + polarity


def packed_products(turned, norm_scale):
    input_count, spec_count, pair_count, slot_count = turned.shape
    arranged = turned.transpose(3, 0, 1, 2)
    stacked = arranged.reshape(slot_count, input_count, spec_count * 2)
    swapped = jnp.stack([-arranged[..., 1], arranged[..., 0]], axis=-1).reshape(
        slot_count, input_count, spec_count * 2
    )
    combined = jnp.concatenate([stacked, swapped], axis=1)
    visible = jnp.einsum("sik,sjk->sij", stacked, combined, preferred_element_type=jnp.float32)
    indices = jnp.arange(input_count)
    upper_half = indices[:, None] <= indices[None, :]
    return (
        jnp.where(upper_half[None], visible[:, :, :input_count], visible[:, :, input_count:])
        * norm_scale
    )


def general_body(samples, history, station_order, channel_order, flagged):
    row_count, local_length = samples.shape
    spec_local = local_length // NFFT
    st_count = lax.axis_size("st")
    tm_count = lax.axis_size("tm")
    pol_count = lax.axis_size("pol")
    slot_share = CH // (st_count * tm_count * pol_count)
    half_slots = CH // pol_count
    lead_length = (TAPS - 1) * NFFT
    earlier = shifted(samples[:, local_length - lead_length :], "tm", 1)
    earlier = jnp.where(lax.axis_index("tm") == 0, history, earlier)
    stream = jnp.concatenate([earlier, samples], axis=1)
    filtered = polyphase(stream, filter_window(TAPS, NFFT), spec_local)
    local_slots = jnp.arange(half_slots)
    global_slots = (
        local_slots // slot_share * (slot_share * pol_count)
        + lax.axis_index("pol") * slot_share
        + local_slots % slot_share
    )
    station_ids = lax.dynamic_slice_in_dim(
        station_order, lax.axis_index("st") * (row_count // 2), row_count // 2
    )
    keeping = jnp.repeat((1 - flagged[station_ids]).astype(jnp.float32), 2)
    product = frame_transform(filtered, channel_order[global_slots], FRAME_A)
    product = product.reshape(row_count, spec_local, 2, half_slots) * keeping[:, None, None, None]
    spectra = product.astype(jnp.bfloat16)
    norm_scale = 1.0 / (spec_local * tm_count)
    input_order = input_rows(station_order)
    turned = lax.all_to_all(
        lax.all_to_all(spectra, "st", split_axis=3, concat_axis=0, tiled=True),
        "tm",
        split_axis=3,
        concat_axis=1,
        tiled=True,
    )
    turned = jnp.take(turned, input_order, axis=0)
    return packed_products(turned, norm_scale)


def fits(samples, mesh):
    st_count, tm_count, pol_count = (mesh.shape[a] for a in AXES)
    rows = samples.shape[0] // st_count
    frames = samples.shape[1] // tm_count // NFFT
    share = CH // (st_count * tm_count * pol_count)
    return (
        rows == ROWS * pol_count
        and frames == 2 * BATCH
        and tm_count == 4
        and share % (2 * GROUP) == 0
        and 256 % share == 0
        and samples.shape[0] % 256 == 0
    )


def solution(mesh):
    def run(samples, history, station_order, channel_order, flagged):
        body = fused_body if fits(samples, mesh) else general_body
        return jax.shard_map(
            body,
            mesh=mesh,
            in_specs=(P("st", "tm"), P("st", None), P(), P(), P()),
            out_specs=P(("st", "tm", "pol"), None, None),
            check_vma=False,
        )(samples, history, station_order, channel_order, flagged)

    return run
```

```python
import functools
import math

import jax
import jax.numpy as jnp
import numpy as np
from jax import lax
from jax.experimental import pallas as pl
from jax.experimental.pallas import tpu as pltpu
from jax.sharding import PartitionSpec as P

NFFT = 8192
FRAME_A = 32
FRAME_B = NFFT // FRAME_A
CH = 2048
TAPS = 4
LEAD = TAPS - 1
HALF_E = FRAME_A // 2
LOW = CH // FRAME_A
AXES = ("st", "tm", "pol")
ROWS = 64
GROUP = 16
PREP = 8
BATCH = 4
PAIRS = BATCH // 2
PER_SLOT = 2 * PAIRS
VMEM = 56 << 20


def np_window():
    length = TAPS * NFFT
    offsets = np.arange(length) + 0.5
    centred = (offsets - 0.5 * length) / NFFT
    tapering = 0.5 - 0.5 * np.cos(offsets * (2.0 * math.pi / length))
    return (np.sinc(centred) * tapering).reshape(TAPS, NFFT).astype(np.float32)


def np_first():
    turns = np.arange(FRAME_A)[:, None] * np.arange(FRAME_A)[None, :] % FRAME_A
    angles = turns * (2.0 * math.pi / FRAME_A)
    cosine = np.cos(angles) / math.sqrt(FRAME_A)
    sine = -np.sin(angles) / math.sqrt(FRAME_A)
    rows = [cosine[0], cosine[HALF_E]]
    for e in range(1, HALF_E):
        rows += [cosine[e], sine[e]]
    return np.kron(np.stack(rows), np.eye(GROUP)).astype(jnp.bfloat16)


def np_twist():
    turns = np.arange(HALF_E + 1)[:, None] * np.arange(FRAME_B)[None, :] % NFFT
    angles = turns * (2.0 * math.pi / NFFT)
    return np.cos(angles).astype(np.float32), np.sin(angles).astype(np.float32)


def np_second():
    f = np.concatenate([np.arange(LOW), FRAME_B - 1 - np.arange(LOW)])
    sign = np.where(np.arange(2 * LOW) < LOW, 1.0, -1.0)[:, None]
    angles = f[:, None] * np.arange(FRAME_B)[None, :] % FRAME_B * (2.0 * math.pi / FRAME_B)
    cosine = np.cos(angles) / math.sqrt(FRAME_B)
    sine = -np.sin(angles) / math.sqrt(FRAME_B)
    top = np.concatenate([cosine, -sine], axis=1)
    bottom = np.concatenate([sine * sign, cosine * sign], axis=1)
    return np.concatenate([top, bottom]).astype(jnp.bfloat16)


def filterbank_body(taps_of, step, refs):
    row_ref, w_ref, c1_ref, cos_ref, sin_ref, w2_ref, outs, y_ref, t_ref, d_ref = refs

    def filter_a(a, carry):
        weights = [w_ref[k : k + 1, pl.ds(pl.multiple_of(a * FRAME_B, FRAME_B), FRAME_B)] for k in range(TAPS)]
        frames = [taps_of(i, a) for i in range(BATCH + LEAD)]
        for t in range(BATCH):
            total = frames[t] * weights[0]
            for k in range(1, TAPS):
                total = total + frames[t + k] * weights[k]
            y_ref[t, pl.ds(pl.multiple_of(a * GROUP, GROUP), GROUP), :] = total.astype(jnp.bfloat16)
        return carry

    lax.fori_loop(0, FRAME_A, filter_a, 0, unroll=2)

    def first_t(t, carry):
        seg = jnp.dot(c1_ref[...], y_ref[t], preferred_element_type=jnp.float32)
        rows = pl.ds(pl.multiple_of(t * ROWS + step * GROUP, GROUP), GROUP)
        for e in range(HALF_E + 1):
            cosine = cos_ref[e : e + 1, :]
            sine = sin_ref[e : e + 1, :]
            if e == 0 or e == HALF_E:
                at = 0 if e == 0 else GROUP
                re = seg[at : at + GROUP]
                twist_re = re * cosine
                twist_im = -(re * sine)
            else:
                at = 2 * e * GROUP
                re = seg[at : at + GROUP]
                im = seg[at + GROUP : at + 2 * GROUP]
                twist_re = re * cosine + im * sine
                twist_im = im * cosine - re * sine
            t_ref[e, rows, 0:FRAME_B] = twist_re.astype(jnp.bfloat16)
            t_ref[e, rows, FRAME_B : 2 * FRAME_B] = twist_im.astype(jnp.bfloat16)
        return carry

    lax.fori_loop(0, BATCH, first_t, 0, unroll=True)

    @pl.when(step == ROWS // GROUP - 1)
    def _():
        for e in range(HALF_E + 1):
            full = lax.dot_general(
                w2_ref[...], t_ref[e], (((1,), (1,)), ((), ())), preferred_element_type=jnp.float32
            )
            for c in range(2):
                for pair in range(PAIRS):
                    start = PER_SLOT + e * 2 * LOW * PER_SLOT + c * PAIRS + pair
                    d_ref[pl.ds(start, 2 * LOW, stride=PER_SLOT), :] = full[
                        c * 2 * LOW : (c + 1) * 2 * LOW, pair * 128 : (pair + 1) * 128
                    ]

        share = sum(out_ref.shape[1] for out_ref in outs) // PER_SLOT
        lower = lax.broadcasted_iota(jnp.int32, (2 * PER_SLOT, 128), 0) < PER_SLOT

        def gather(peer, carry):
            slot = peer * share
            for out_ref in outs:
                for at in range(0, out_ref.shape[1], 4 * PER_SLOT):
                    halves = []
                    for k in (0, 2):
                        one = d_ref[pl.ds(row_ref[slot + k] + PER_SLOT, 2 * PER_SLOT), :]
                        two = d_ref[pl.ds(row_ref[slot + k + 1], 2 * PER_SLOT), :]
                        halves.append(jnp.where(lower, one, two))
                    slot = slot + 4
                    out_ref[peer, at : at + 4 * PER_SLOT, :] = jnp.concatenate(halves).astype(jnp.bfloat16)
            return carry

        lax.fori_loop(0, outs[0].shape[0], gather, 0)


def late_kernel(place_ref, row_ref, x_ref, w_ref, c1_ref, cos_ref, sin_ref, w2_ref, *rest):
    outs, (y_ref, t_ref, d_ref) = rest[:-3], rest[-3:]
    first = x_ref.shape[1] // NFFT - BATCH

    def taps_of(i, a):
        at = (first - LEAD + i) * NFFT
        return x_ref[:, pl.ds(pl.multiple_of(at + a * FRAME_B, FRAME_B), FRAME_B)].astype(jnp.float32)

    refs = (row_ref, w_ref, c1_ref, cos_ref, sin_ref, w2_ref, outs, y_ref, t_ref, d_ref)
    filterbank_body(taps_of, pl.program_id(0), refs)


def early_kernel(
    place_ref, row_ref, x_ref, halo_ref, history_ref, w_ref, c1_ref, cos_ref, sin_ref, w2_ref, *rest
):
    outs, (y_ref, t_ref, d_ref) = rest[:-3], rest[-3:]
    opening = place_ref[1] == 0

    def taps_of(i, a):
        if i >= LEAD:
            at = pl.multiple_of((i - LEAD) * NFFT + a * FRAME_B, FRAME_B)
            return x_ref[:, pl.ds(at, FRAME_B)].astype(jnp.float32)
        at = pl.multiple_of(i * NFFT + a * FRAME_B, FRAME_B)
        mine = halo_ref[:, pl.ds(at, FRAME_B)].astype(jnp.float32)
        old = history_ref[:, pl.ds(at, FRAME_B)].astype(jnp.float32)
        return jnp.where(opening, old, mine)

    refs = (row_ref, w_ref, c1_ref, cos_ref, sin_ref, w2_ref, outs, y_ref, t_ref, d_ref)
    filterbank_body(taps_of, pl.program_id(0), refs)


def filterbank(kernel, name, peers, parts, place, rows, streams, stream_specs, consts):
    whole = [pl.BlockSpec(c.shape, lambda i, p, r: (0, 0)) for c in consts]
    outs = [jax.ShapeDtypeStruct((peers, part * PER_SLOT, 128), jnp.bfloat16) for part in parts]
    return pl.pallas_call(
        kernel,
        out_shape=outs,
        grid_spec=pltpu.PrefetchScalarGridSpec(
            num_scalar_prefetch=2,
            grid=(ROWS // GROUP,),
            in_specs=stream_specs + whole,
            out_specs=[pl.BlockSpec(out.shape, lambda i, p, r: (0, 0, 0)) for out in outs],
            scratch_shapes=[
                pltpu.VMEM((BATCH, FRAME_A * GROUP, FRAME_B), jnp.bfloat16),
                pltpu.VMEM((HALF_E + 1, BATCH * ROWS, 2 * FRAME_B), jnp.bfloat16),
                pltpu.VMEM(((HALF_E + 1) * 2 * LOW * PER_SLOT + 2 * PER_SLOT, 128), jnp.float32),
            ],
        ),
        cost_estimate=pl.CostEstimate(flops=12 * 10**9, bytes_accessed=16 << 20, transcendentals=0),
        compiler_params=pltpu.CompilerParams(
            dimension_semantics=("arbitrary",), vmem_limit_bytes=VMEM
        ),
        name=name,
    )(place, rows, *streams, *consts)


def order_inputs(source, perm_ref, lhs_ref, z_ref, sizes, span):
    st_count, tm_count, pol_count = sizes
    half = 128 // 2
    for tm in range(tm_count):
        for st in range(st_count):
            blocks = [source[(st * tm_count + tm) * pol_count + pol] for pol in range(pol_count)]
            lanes = slice(st * pol_count * half, (st + 1) * pol_count * half)
            for odd in range(2):
                row = (odd * tm_count + tm) * span
                lhs_ref[row : row + span, lanes] = jnp.concatenate(
                    [block[:, odd * half : (odd + 1) * half] for block in blocks], axis=1
                )
    turned = jnp.dot(lhs_ref[...], perm_ref[...], preferred_element_type=jnp.float32)
    for j in range(z_ref.shape[0]):
        z_ref[j] = turned[:, j * 128 : (j + 1) * 128]


def slot_rows(z_ref, slot, c, span, count):
    tiles = [
        jnp.concatenate(
            [
                z_ref[j, pl.ds(slot * PER_SLOT + c * PAIRS + pair, count, stride=span), :]
                for j in range(z_ref.shape[0])
            ],
            axis=1,
        )
        for pair in range(PAIRS)
    ]
    return jnp.concatenate(tiles, axis=0).astype(jnp.bfloat16)


def order_kernel(sizes, late_ref, perm_ref, out_ref, lhs_ref, z_ref):
    slots = out_ref.shape[0]
    span = slots * PER_SLOT
    order_inputs(late_ref, perm_ref, lhs_ref, z_ref, sizes, span)
    count = 2 * sizes[1]
    for slot in range(slots):
        for c in range(2):
            out_ref[slot, c * PAIRS * count : (c + 1) * PAIRS * count, :] = slot_rows(
                z_ref, slot, c, span, count
            )


def order_late(share, sizes, late, perm):
    peers = late.shape[0]
    inputs = perm.shape[1]
    span = GROUP * PER_SLOT
    rows = 2 * sizes[1] * span
    depth = 2 * sizes[1] * PER_SLOT
    return pl.pallas_call(
        functools.partial(order_kernel, sizes),
        out_shape=jax.ShapeDtypeStruct((share, depth, inputs), jnp.bfloat16),
        grid=(share // GROUP,),
        in_specs=[
            pl.BlockSpec((peers, span, 128), lambda i: (0, i, 0)),
            pl.BlockSpec(perm.shape, lambda i: (0, 0)),
        ],
        out_specs=pl.BlockSpec((GROUP, depth, inputs), lambda i: (i, 0, 0)),
        scratch_shapes=[
            pltpu.VMEM((rows, inputs), jnp.bfloat16),
            pltpu.VMEM((inputs // 128, rows, 128), jnp.float32),
        ],
        cost_estimate=pl.CostEstimate(flops=8 * 10**9, bytes_accessed=4 << 20, transcendentals=0),
        compiler_params=pltpu.CompilerParams(
            dimension_semantics=("arbitrary",), vmem_limit_bytes=VMEM
        ),
        name="order_late",
    )(late, perm)


def correlate_kernel(scale, sizes, per_step, *refs):
    late_ref, early_ref, perm_ref = refs[:3]
    out_ref, lhs_ref, z_ref, ordered_ref = refs[-4:]
    step = pl.program_id(0)
    inputs = out_ref.shape[1]
    span = PREP * PER_SLOT
    count = 2 * sizes[1]
    depth = PAIRS * count

    @pl.when(step % (PREP // per_step) == 0)
    def _():
        order_inputs(early_ref, perm_ref, lhs_ref, z_ref, sizes, span)
        for slot in range(PREP):
            for c in range(2):
                ordered_ref[slot, c * depth : (c + 1) * depth, :] = slot_rows(z_ref, slot, c, span, count)

    mid = inputs // 2
    tall = lax.broadcasted_iota(jnp.int32, (mid, mid), 0)
    wide = lax.broadcasted_iota(jnp.int32, (mid, mid), 1)
    upper = tall <= wide

    def one(i, carry):
        slot = lax.rem(step, PREP // per_step) * per_step + i
        early = ordered_ref[slot]
        late = late_ref[i]
        z = jnp.concatenate([early, late], axis=0)
        turned = jnp.concatenate(
            [-early[depth:], early[:depth], -late[depth:], late[:depth]], axis=0
        )
        left = z.T
        dot = functools.partial(jnp.dot, preferred_element_type=jnp.float32)
        for h in range(2):
            here = slice(h * mid, (h + 1) * mid)
            re = dot(left[here], z[:, here])
            im = dot(left[here], turned[:, here])
            out_ref[i, here, here] = jnp.where(upper, re, im) * scale
        out_ref[i, :mid, mid:] = dot(left[:mid], z[:, mid:]) * scale
        out_ref[i, mid:, :mid] = dot(left[mid:], turned[:, :mid]) * scale
        return carry

    lax.fori_loop(0, per_step, one, 0, unroll=True)


def correlate(start, part, share, inputs, scale, sizes, late, early, perm, before):
    per_step = 4
    prep = PREP // per_step
    peers = early.shape[0]
    depth = late.shape[1]
    span = PREP * PER_SLOT
    rows = 2 * sizes[1] * span
    in_specs = [
        pl.BlockSpec((per_step, depth, inputs), lambda i: (start // per_step + i, 0, 0)),
        pl.BlockSpec((peers, span, 128), lambda i: (0, i // prep, 0)),
        pl.BlockSpec(perm.shape, lambda i: (0, 0)),
    ]
    operands = [late, early, perm]
    aliases = {}
    if before is not None:
        in_specs.append(pl.BlockSpec(memory_space=pl.ANY))
        operands.append(before)
        aliases = {3: 0}
    return pl.pallas_call(
        functools.partial(correlate_kernel, scale, sizes, per_step),
        out_shape=jax.ShapeDtypeStruct((share, inputs, inputs), jnp.float32),
        grid=(part // per_step,),
        in_specs=in_specs,
        out_specs=pl.BlockSpec((per_step, inputs, inputs), lambda i: (start // per_step + i, 0, 0)),
        scratch_shapes=[
            pltpu.VMEM((rows, inputs), jnp.bfloat16),
            pltpu.VMEM((inputs // 128, rows, 128), jnp.float32),
            pltpu.VMEM((PREP, depth, inputs), jnp.bfloat16),
        ],
        input_output_aliases=aliases,
        cost_estimate=pl.CostEstimate(
            flops=part * 12 * 10**7, bytes_accessed=part * inputs * inputs * 4, transcendentals=0
        ),
        compiler_params=pltpu.CompilerParams(
            dimension_semantics=("arbitrary",), vmem_limit_bytes=VMEM
        ),
        name="correlate",
    )(*operands)


def fused_body(samples, history, station_order, channel_order, flagged):
    row_count, local_length = samples.shape
    spec_local = local_length // NFFT
    st_count = lax.axis_size("st")
    tm_count = lax.axis_size("tm")
    pol_count = lax.axis_size("pol")
    peers = st_count * tm_count * pol_count
    share = CH // peers
    inputs = row_count * st_count
    pol = lax.axis_index("pol")
    place = jnp.stack([pol, lax.axis_index("tm")]).astype(jnp.int32)

    ending = lax.dynamic_slice(
        samples, (pol * ROWS, local_length - LEAD * NFFT), (ROWS, LEAD * NFFT)
    )
    halo = lax.ppermute(ending, "tm", [(i, i + 1) for i in range(tm_count - 1)])

    e, f = channel_order % FRAME_A, channel_order // FRAME_A
    row = jnp.minimum(e, FRAME_A - e) * (2 * LOW) + jnp.where(e > HALF_E, LOW, 0) + f
    rows = (row * PER_SLOT).astype(jnp.int32)
    cosine, sine = np_twist()
    consts = [jnp.asarray(c) for c in (np_window(), np_first(), cosine, sine, np_second())]

    groups = ROWS // GROUP
    late = filterbank(
        late_kernel, "filterbank_late", peers, [share], place, rows, [samples],
        [pl.BlockSpec((GROUP, local_length), lambda i, p, r: (p[0] * groups + i, 0))],
        consts,
    )
    late = lax.all_to_all(late[0], AXES, split_axis=0, concat_axis=0, tiled=True)
    tail = share * 3 // 8
    parts = [share - tail, tail]
    early = filterbank(
        early_kernel, "filterbank_early", peers, parts, place, rows, [samples, halo, history],
        [
            pl.BlockSpec((GROUP, BATCH * NFFT), lambda i, p, r: (p[0] * groups + i, 0)),
            pl.BlockSpec((GROUP, LEAD * NFFT), lambda i, p, r: (i, 0)),
            pl.BlockSpec((GROUP, LEAD * NFFT), lambda i, p, r: (p[0] * groups + i, 0)),
        ],
        consts,
    )
    line = jnp.arange(inputs)
    target = 2 * jnp.repeat(station_order, 2) + line % 2
    keep = 1 - jnp.repeat(flagged, 2)
    perm = ((target[:, None] == line[None, :]) & (keep[None, :] == 1)).astype(jnp.bfloat16)

    *early, perm = lax.optimization_barrier((*early, perm))
    sizes = (st_count, tm_count, pol_count)
    first = lax.all_to_all(early[0], AXES, split_axis=0, concat_axis=0, tiled=True)
    late = order_late(share, sizes, late, perm)
    rest, late = lax.optimization_barrier((early[1], late))
    rest = lax.all_to_all(rest, AXES, split_axis=0, concat_axis=0, tiled=True)

    scale = 1.0 / (spec_local * tm_count)
    out = None
    start = 0
    for part, arrived in zip(parts, (first, rest)):
        out = correlate(start, part, share, inputs, scale, sizes, late, arrived, perm, out)
        start += part
    return out


def shifted(array, axis, by):
    peers = lax.axis_size(axis)
    pairs = [(i, i + by) for i in range(peers) if 0 <= i + by < peers]
    return lax.ppermute(array, axis, pairs)


def filter_window(tap_count, frame_size):
    length = tap_count * frame_size
    offsets = jnp.arange(length).astype(jnp.float32) + 0.5
    centred = (offsets - 0.5 * length) / frame_size
    tapering = 0.5 - 0.5 * jnp.cos(offsets * (2.0 * math.pi / length))
    return (jnp.sinc(centred) * tapering).reshape(tap_count, frame_size)


def polyphase(row_block, weights, spec_count):
    row_total = row_block.shape[0]
    tap_count, frame_size = weights.shape
    running = jnp.zeros((row_total, spec_count, frame_size), jnp.float32)
    for tap_index in range(tap_count):
        section = row_block[:, tap_index * frame_size : (tap_index + spec_count) * frame_size]
        section = section.reshape(row_total, spec_count, frame_size)
        running = running + section.astype(jnp.float32) * weights[tap_index]
    return running.astype(jnp.bfloat16).reshape(row_total * spec_count, frame_size)


def trig_pair(left, right, modulus, amplitude):
    turn_count = left[:, None] * right[None, :] % modulus
    angles = turn_count.astype(jnp.float32) * (2.0 * math.pi / modulus)
    cosine = (jnp.cos(angles) * amplitude).astype(jnp.bfloat16)
    sine_part = (-(jnp.sin(angles) * amplitude)).astype(jnp.bfloat16)
    return (cosine, sine_part)


def product_low(form, left, right):
    return jnp.einsum(form, left, right, preferred_element_type=jnp.float32)


def frame_transform(filtered, channels, first_len):
    row_total, frame_size = filtered.shape
    second_len = frame_size // first_len
    half_len = second_len // 2
    first_idx = jnp.arange(first_len)
    second_idx = jnp.arange(second_len)
    half_idx = jnp.arange(half_len)
    first_cos, first_sin = trig_pair(first_idx, first_idx, first_len, 1.0 / math.sqrt(first_len))
    blocks = filtered.reshape(row_total, first_len, second_len)
    segment_re = product_low("rab,ae->reb", blocks, first_cos)
    segment_im = product_low("rab,ae->reb", blocks, first_sin)
    twist_turns = first_idx[:, None] * second_idx[None, :] % frame_size
    twist_angles = twist_turns.astype(jnp.float32) * (2.0 * math.pi / frame_size)
    twist_cos = jnp.cos(twist_angles)
    twist_sin = jnp.sin(twist_angles)
    twist_re = (segment_re * twist_cos + segment_im * twist_sin).astype(jnp.bfloat16)
    twist_im = (segment_im * twist_cos - segment_re * twist_sin).astype(jnp.bfloat16)
    second_cos, second_sin = trig_pair(
        second_idx, half_idx, second_len, 1.0 / math.sqrt(second_len)
    )
    full_re = product_low("reb,bf->ref", twist_re, second_cos) - product_low(
        "reb,bf->ref", twist_im, second_sin
    )
    full_im = product_low("reb,bf->ref", twist_re, second_sin) + product_low(
        "reb,bf->ref", twist_im, second_cos
    )
    column = channels % first_len * half_len + channels // first_len
    flat_re = jnp.take(full_re.reshape(row_total, first_len * half_len), column, axis=1)
    flat_im = jnp.take(full_im.reshape(row_total, first_len * half_len), column, axis=1)
    return jnp.stack([flat_re, flat_im], axis=1)


def input_rows(station_order):
    station_total = station_order.shape[0]
    inverse = (
        jnp.zeros((station_total,), jnp.int32).at[station_order].set(jnp.arange(station_total))
    )
    polarity = jnp.tile(jnp.arange(2), station_total)
    return 2 * jnp.repeat(inverse, 2) + polarity


def packed_products(turned, norm_scale):
    input_count, spec_count, pair_count, slot_count = turned.shape
    arranged = turned.transpose(3, 0, 1, 2)
    stacked = arranged.reshape(slot_count, input_count, spec_count * 2)
    swapped = jnp.stack([-arranged[..., 1], arranged[..., 0]], axis=-1).reshape(
        slot_count, input_count, spec_count * 2
    )
    combined = jnp.concatenate([stacked, swapped], axis=1)
    visible = jnp.einsum("sik,sjk->sij", stacked, combined, preferred_element_type=jnp.float32)
    indices = jnp.arange(input_count)
    upper_half = indices[:, None] <= indices[None, :]
    return (
        jnp.where(upper_half[None], visible[:, :, :input_count], visible[:, :, input_count:])
        * norm_scale
    )


def general_body(samples, history, station_order, channel_order, flagged):
    row_count, local_length = samples.shape
    spec_local = local_length // NFFT
    st_count = lax.axis_size("st")
    tm_count = lax.axis_size("tm")
    pol_count = lax.axis_size("pol")
    slot_share = CH // (st_count * tm_count * pol_count)
    half_slots = CH // pol_count
    lead_length = (TAPS - 1) * NFFT
    earlier = shifted(samples[:, local_length - lead_length :], "tm", 1)
    earlier = jnp.where(lax.axis_index("tm") == 0, history, earlier)
    stream = jnp.concatenate([earlier, samples], axis=1)
    filtered = polyphase(stream, filter_window(TAPS, NFFT), spec_local)
    local_slots = jnp.arange(half_slots)
    global_slots = (
        local_slots // slot_share * (slot_share * pol_count)
        + lax.axis_index("pol") * slot_share
        + local_slots % slot_share
    )
    station_ids = lax.dynamic_slice_in_dim(
        station_order, lax.axis_index("st") * (row_count // 2), row_count // 2
    )
    keeping = jnp.repeat((1 - flagged[station_ids]).astype(jnp.float32), 2)
    product = frame_transform(filtered, channel_order[global_slots], FRAME_A)
    product = product.reshape(row_count, spec_local, 2, half_slots) * keeping[:, None, None, None]
    spectra = product.astype(jnp.bfloat16)
    norm_scale = 1.0 / (spec_local * tm_count)
    input_order = input_rows(station_order)
    turned = lax.all_to_all(
        lax.all_to_all(spectra, "st", split_axis=3, concat_axis=0, tiled=True),
        "tm",
        split_axis=3,
        concat_axis=1,
        tiled=True,
    )
    turned = jnp.take(turned, input_order, axis=0)
    return packed_products(turned, norm_scale)


def fits(samples, mesh):
    st_count, tm_count, pol_count = (mesh.shape[a] for a in AXES)
    rows = samples.shape[0] // st_count
    frames = samples.shape[1] // tm_count // NFFT
    share = CH // (st_count * tm_count * pol_count)
    return (
        rows == ROWS * pol_count
        and frames == 2 * BATCH
        and tm_count == 4
        and pol_count == 2
        and share % (8 * PREP) == 0
        and samples.shape[0] % 256 == 0
    )


def solution(mesh):
    def run(samples, history, station_order, channel_order, flagged):
        body = fused_body if fits(samples, mesh) else general_body
        return jax.shard_map(
            body,
            mesh=mesh,
            in_specs=(P("st", "tm"), P("st", None), P(), P(), P()),
            out_specs=P(("st", "tm", "pol"), None, None),
            check_vma=False,
        )(samples, history, station_order, channel_order, flagged)

    return run
```

```python
import functools
import math

import jax
import jax.numpy as jnp
import numpy as np
from jax import lax
from jax.experimental import pallas as pl
from jax.experimental.pallas import tpu as pltpu
from jax.sharding import PartitionSpec as P

NFFT = 8192
FRAME_A = 32
FRAME_B = NFFT // FRAME_A
CH = 2048
TAPS = 4
LEAD = TAPS - 1
HALF_E = FRAME_A // 2
LOW = CH // FRAME_A
AXES = ("st", "tm", "pol")
ROWS = 64
GROUP = 16
PREP = 8
BATCHED = 2
UNROLLED = 3
BATCH = 4
PAIRS = BATCH // 2
PER_SLOT = 2 * PAIRS
VMEM = 62 << 20
BANK_VMEM = 56 << 20


def np_window():
    length = TAPS * NFFT
    offsets = np.arange(length) + 0.5
    centred = (offsets - 0.5 * length) / NFFT
    tapering = 0.5 - 0.5 * np.cos(offsets * (2.0 * math.pi / length))
    return (np.sinc(centred) * tapering).reshape(TAPS, NFFT).astype(np.float32)


def np_first():
    turns = np.arange(FRAME_A)[:, None] * np.arange(FRAME_A)[None, :] % FRAME_A
    angles = turns * (2.0 * math.pi / FRAME_A)
    cosine = np.cos(angles) / math.sqrt(FRAME_A)
    sine = -np.sin(angles) / math.sqrt(FRAME_A)
    rows = [cosine[0], cosine[HALF_E]]
    for e in range(1, HALF_E):
        rows += [cosine[e], sine[e]]
    return np.kron(np.stack(rows), np.eye(GROUP)).astype(jnp.bfloat16)


def np_twist():
    turns = np.arange(HALF_E + 1)[:, None] * np.arange(FRAME_B)[None, :] % NFFT
    angles = turns * (2.0 * math.pi / NFFT)
    return np.cos(angles).astype(np.float32), np.sin(angles).astype(np.float32)


def np_second():
    f = np.concatenate([np.arange(LOW), FRAME_B - 1 - np.arange(LOW)])
    sign = np.where(np.arange(2 * LOW) < LOW, 1.0, -1.0)[:, None]
    angles = f[:, None] * np.arange(FRAME_B)[None, :] % FRAME_B * (2.0 * math.pi / FRAME_B)
    cosine = np.cos(angles) / math.sqrt(FRAME_B)
    sine = -np.sin(angles) / math.sqrt(FRAME_B)
    top = np.concatenate([cosine, -sine], axis=1)
    bottom = np.concatenate([sine * sign, cosine * sign], axis=1)
    return np.concatenate([top, bottom]).astype(jnp.bfloat16)


def filterbank_body(sources, step, refs):
    row_ref, w_ref, c1_ref, cos_ref, sin_ref, w2_ref, outs, y_ref, t_ref, d_ref = refs

    def filter_a(taps_of, a, carry):
        weights = [w_ref[k : k + 1, pl.ds(pl.multiple_of(a * FRAME_B, FRAME_B), FRAME_B)] for k in range(TAPS)]
        frames = [taps_of(i, a) for i in range(BATCH + LEAD)]
        for t in range(BATCH):
            total = frames[t] * weights[0]
            for k in range(1, TAPS):
                total = total + frames[t + k] * weights[k]
            y_ref[t, pl.ds(pl.multiple_of(a * GROUP, GROUP), GROUP), :] = total.astype(jnp.bfloat16)
        return carry

    if len(sources) == 1:
        lax.fori_loop(0, FRAME_A, functools.partial(filter_a, sources[0]), 0, unroll=2)
    else:
        opening = row_ref[CH + 1] == 0

        @pl.when(opening)
        def _():
            lax.fori_loop(0, FRAME_A, functools.partial(filter_a, sources[0]), 0, unroll=2)

        @pl.when(jnp.logical_not(opening))
        def _():
            lax.fori_loop(0, FRAME_A, functools.partial(filter_a, sources[1]), 0, unroll=2)

    def first_t(t, carry):
        seg = jnp.dot(c1_ref[...], y_ref[t], preferred_element_type=jnp.float32)
        rows = pl.ds(pl.multiple_of(t * ROWS + step * GROUP, GROUP), GROUP)
        for e in range(HALF_E + 1):
            cosine = cos_ref[e : e + 1, :]
            sine = sin_ref[e : e + 1, :]
            if e == 0 or e == HALF_E:
                at = 0 if e == 0 else GROUP
                re = seg[at : at + GROUP]
                twist_re = re * cosine
                twist_im = -(re * sine)
            else:
                at = 2 * e * GROUP
                re = seg[at : at + GROUP]
                im = seg[at + GROUP : at + 2 * GROUP]
                twist_re = re * cosine + im * sine
                twist_im = im * cosine - re * sine
            t_ref[e, rows, 0:FRAME_B] = twist_re.astype(jnp.bfloat16)
            t_ref[e, rows, FRAME_B : 2 * FRAME_B] = twist_im.astype(jnp.bfloat16)
        return carry

    lax.fori_loop(0, BATCH, first_t, 0, unroll=True)

    @pl.when(step == ROWS // GROUP - 1)
    def _():
        for e in range(HALF_E + 1):
            full = lax.dot_general(
                w2_ref[...], t_ref[e], (((1,), (1,)), ((), ())), preferred_element_type=jnp.float32
            )
            for c in range(2):
                for pair in range(PAIRS):
                    start = PER_SLOT + e * 2 * LOW * PER_SLOT + c * PAIRS + pair
                    d_ref[pl.ds(start, 2 * LOW, stride=PER_SLOT), :] = full[
                        c * 2 * LOW : (c + 1) * 2 * LOW, pair * 128 : (pair + 1) * 128
                    ]

        share = sum(out_ref.shape[1] for out_ref in outs) // PER_SLOT
        lower = lax.broadcasted_iota(jnp.int32, (2 * PER_SLOT, 128), 0) < PER_SLOT

        def gather(peer, carry):
            slot = peer * share
            for out_ref in outs:
                for at in range(0, out_ref.shape[1], 4 * PER_SLOT):
                    halves = []
                    for k in (0, 2):
                        one = d_ref[pl.ds(row_ref[slot + k] + PER_SLOT, 2 * PER_SLOT), :]
                        two = d_ref[pl.ds(row_ref[slot + k + 1], 2 * PER_SLOT), :]
                        halves.append(jnp.where(lower, one, two))
                    slot = slot + 4
                    out_ref[peer, at : at + 4 * PER_SLOT, :] = jnp.concatenate(halves).astype(jnp.bfloat16)
            return carry

        lax.fori_loop(0, outs[0].shape[0], gather, 0)


def late_kernel(row_ref, x_ref, w_ref, c1_ref, cos_ref, sin_ref, w2_ref, *rest):
    outs, (y_ref, t_ref, d_ref) = rest[:-3], rest[-3:]
    first = x_ref.shape[1] // NFFT - BATCH

    def taps_of(i, a):
        at = (first - LEAD + i) * NFFT
        return x_ref[:, pl.ds(pl.multiple_of(at + a * FRAME_B, FRAME_B), FRAME_B)].astype(jnp.float32)

    refs = (row_ref, w_ref, c1_ref, cos_ref, sin_ref, w2_ref, outs, y_ref, t_ref, d_ref)
    filterbank_body([taps_of], pl.program_id(0), refs)


def early_kernel(
    row_ref, x_ref, halo_ref, history_ref, w_ref, c1_ref, cos_ref, sin_ref, w2_ref, *rest
):
    outs, (y_ref, t_ref, d_ref) = rest[:-3], rest[-3:]

    def taps_from(ahead_ref):
        def taps_of(i, a):
            source, at = (x_ref, i - LEAD) if i >= LEAD else (ahead_ref, i)
            at = pl.multiple_of(at * NFFT + a * FRAME_B, FRAME_B)
            return source[:, pl.ds(at, FRAME_B)].astype(jnp.float32)

        return taps_of

    refs = (row_ref, w_ref, c1_ref, cos_ref, sin_ref, w2_ref, outs, y_ref, t_ref, d_ref)
    filterbank_body([taps_from(history_ref), taps_from(halo_ref)], pl.program_id(0), refs)


def filterbank(kernel, name, peers, parts, rows, streams, stream_specs, consts):
    whole = [pl.BlockSpec(c.shape, lambda i, r: (0, 0)) for c in consts]
    outs = [jax.ShapeDtypeStruct((peers, part * PER_SLOT, 128), jnp.bfloat16) for part in parts]
    return pl.pallas_call(
        kernel,
        out_shape=outs,
        grid_spec=pltpu.PrefetchScalarGridSpec(
            num_scalar_prefetch=1,
            grid=(ROWS // GROUP,),
            in_specs=stream_specs + whole,
            out_specs=[pl.BlockSpec(out.shape, lambda i, r: (0, 0, 0)) for out in outs],
            scratch_shapes=[
                pltpu.VMEM((BATCH, FRAME_A * GROUP, FRAME_B), jnp.bfloat16),
                pltpu.VMEM((HALF_E + 1, BATCH * ROWS, 2 * FRAME_B), jnp.bfloat16),
                pltpu.VMEM(((HALF_E + 1) * 2 * LOW * PER_SLOT + 2 * PER_SLOT, 128), jnp.float32),
            ],
        ),
        cost_estimate=pl.CostEstimate(flops=12 * 10**9, bytes_accessed=16 << 20, transcendentals=0),
        compiler_params=pltpu.CompilerParams(
            dimension_semantics=("arbitrary",), vmem_limit_bytes=BANK_VMEM
        ),
        name=name,
    )(rows, *streams, *consts)


def order_inputs(source, perm_ref, lhs_ref, z_ref, sizes, span):
    st_count, tm_count, pol_count = sizes
    half = 128 // 2
    for tm in range(tm_count):
        for st in range(st_count):
            blocks = [source[(st * tm_count + tm) * pol_count + pol] for pol in range(pol_count)]
            lanes = slice(st * pol_count * half, (st + 1) * pol_count * half)
            for odd in range(2):
                row = (odd * tm_count + tm) * span
                lhs_ref[row : row + span, lanes] = jnp.concatenate(
                    [block[:, odd * half : (odd + 1) * half] for block in blocks], axis=1
                )
    turned = jnp.dot(lhs_ref[...], perm_ref[...], preferred_element_type=jnp.float32)
    for j in range(z_ref.shape[0]):
        z_ref[j] = turned[:, j * 128 : (j + 1) * 128]


def slot_rows(z_ref, slot, c, span, count):
    tiles = [
        jnp.concatenate(
            [
                z_ref[j, pl.ds(slot * PER_SLOT + c * PAIRS + pair, count, stride=span), :]
                for j in range(z_ref.shape[0])
            ],
            axis=1,
        )
        for pair in range(PAIRS)
    ]
    return jnp.concatenate(tiles, axis=0).astype(jnp.bfloat16)


def order_kernel(sizes, late_ref, perm_ref, out_ref, lhs_ref, z_ref):
    slots = out_ref.shape[0]
    span = slots * PER_SLOT
    order_inputs(late_ref, perm_ref, lhs_ref, z_ref, sizes, span)
    count = 2 * sizes[1]
    for slot in range(slots):
        for c in range(2):
            out_ref[slot, c * PAIRS * count : (c + 1) * PAIRS * count, :] = slot_rows(
                z_ref, slot, c, span, count
            )


def order_late(part, sizes, late, perm):
    peers = late.shape[0]
    inputs = perm.shape[1]
    span = PREP * PER_SLOT
    rows = 2 * sizes[1] * span
    depth = 2 * sizes[1] * PER_SLOT
    return pl.pallas_call(
        functools.partial(order_kernel, sizes),
        out_shape=jax.ShapeDtypeStruct((part, depth, inputs), jnp.bfloat16),
        grid=(part // PREP,),
        in_specs=[
            pl.BlockSpec((peers, span, 128), lambda i: (0, i, 0)),
            pl.BlockSpec(perm.shape, lambda i: (0, 0)),
        ],
        out_specs=pl.BlockSpec((PREP, depth, inputs), lambda i: (i, 0, 0)),
        scratch_shapes=[
            pltpu.VMEM((rows, inputs), jnp.bfloat16),
            pltpu.VMEM((inputs // 128, rows, 128), jnp.float32),
        ],
        cost_estimate=pl.CostEstimate(flops=8 * 10**9, bytes_accessed=4 << 20, transcendentals=0),
        compiler_params=pltpu.CompilerParams(
            dimension_semantics=("arbitrary",), vmem_limit_bytes=VMEM
        ),
        name="order_late",
    )(late, perm)


def correlate_kernel(scale, sizes, start, *refs):
    late_ref, arrived_ref, perm_ref = refs[:3]
    out_ref, lhs_ref, z_ref, ordered_ref, buffer_ref, sems = refs[-6:]
    inputs = perm_ref.shape[1]
    span = PREP * PER_SLOT
    count = 2 * sizes[1]
    depth = PAIRS * count
    batches, batch = buffer_ref.shape[:2]
    tile = 128
    tall = lax.broadcasted_iota(jnp.int32, (tile, tile), 0)
    wide = lax.broadcasted_iota(jnp.int32, (tile, tile), 1)
    upper = tall <= wide

    def leave(group, k):
        first = start + group * PREP + k * batch
        return pltpu.make_async_copy(
            buffer_ref.at[k], out_ref.at[pl.ds(first, batch)], sems.at[k]
        )

    def products(z, turned, left, into):
        for at in range(0, inputs, tile):
            rows = slice(at, at + tile)
            sides = jnp.concatenate([turned[:, : at + tile], z[:, at:]], axis=1)
            both = jnp.dot(left[rows], sides, preferred_element_type=jnp.float32) * scale
            if at > 0:
                into[rows, :at] = both[:, :at]
            into[rows, rows] = jnp.where(
                upper, both[:, at + tile : at + 2 * tile], both[:, at : at + tile]
            )
            if at + tile < inputs:
                into[rows, at + tile :] = both[:, at + 2 * tile :]

    def order(group, parity):
        source = arrived_ref.at[:, pl.ds(pl.multiple_of(group * span, span), span), :]
        order_inputs(source, perm_ref, lhs_ref, z_ref, sizes, span)
        for slot in range(PREP):
            for c in range(2):
                ordered_ref[parity, slot, c * depth : (c + 1) * depth, :] = slot_rows(
                    z_ref, slot, c, span, count
                )

    groups = late_ref.shape[0] // PREP

    def work(group, parity, fresh, following):
        for k in range(batches):
            if not fresh:
                leave(group - 1, k).wait()
            if k == 1 and following is not None:
                order(following, 1 - parity)
            for i in range(batch):
                slot = k * batch + i
                z = jnp.concatenate([ordered_ref[parity, slot], late_ref[group * PREP + slot]], axis=0)
                turned = []
                for at in range(0, z.shape[0], 2 * depth):
                    turned += [-z[at + depth : at + 2 * depth], z[at : at + depth]]
                turned = jnp.concatenate(turned, axis=0)
                products(z, turned, z.T, buffer_ref.at[k, i])
            leave(group, k).start()

    order(0, 0)
    if groups <= UNROLLED:
        for group in range(groups):
            work(group, group % 2, group == 0, group + 1 if group + 1 < groups else None)
    else:

        def follow(group, carry):
            work(group, lax.rem(group, 2), False, jnp.minimum(group + 1, groups - 1))
            return carry

        work(0, 0, True, 1)
        lax.fori_loop(1, groups, follow, 0)
    for k in range(batches):
        leave(groups - 1, k).wait()


def correlate(start, part, share, inputs, scale, sizes, late, arrived, perm, before):
    depth = late.shape[1]
    rows = 2 * sizes[1] * PREP * PER_SLOT
    operands = [late, arrived, perm]
    in_specs = [
        pl.BlockSpec((pl.Element(part), pl.Element(depth), pl.Element(inputs)), lambda i: (start, 0, 0)),
        pl.BlockSpec(arrived.shape, lambda i: (0, 0, 0)),
        pl.BlockSpec(perm.shape, lambda i: (0, 0)),
    ]
    aliases = {}
    if before is not None:
        in_specs.append(pl.BlockSpec(memory_space=pl.ANY))
        aliases = {len(operands): 0}
        operands.append(before)
    return pl.pallas_call(
        functools.partial(correlate_kernel, scale, sizes, start),
        out_shape=jax.ShapeDtypeStruct((share, inputs, inputs), jnp.float32),
        grid=(1,),
        in_specs=in_specs,
        out_specs=pl.BlockSpec(memory_space=pl.ANY),
        scratch_shapes=[
            pltpu.VMEM((rows, inputs), jnp.bfloat16),
            pltpu.VMEM((inputs // 128, rows, 128), jnp.float32),
            pltpu.VMEM((2, PREP, depth, inputs), jnp.bfloat16),
            pltpu.VMEM((PREP // BATCHED, BATCHED, inputs, inputs), jnp.float32),
            pltpu.SemaphoreType.DMA((PREP // BATCHED,)),
        ],
        input_output_aliases=aliases,
        cost_estimate=pl.CostEstimate(
            flops=part * 12 * 10**7, bytes_accessed=part * inputs * inputs * 4, transcendentals=0
        ),
        compiler_params=pltpu.CompilerParams(
            dimension_semantics=("arbitrary",), vmem_limit_bytes=VMEM
        ),
        name="correlate",
    )(*operands)


def fused_body(samples, history, station_order, channel_order, flagged):
    row_count, local_length = samples.shape
    spec_local = local_length // NFFT
    st_count = lax.axis_size("st")
    tm_count = lax.axis_size("tm")
    pol_count = lax.axis_size("pol")
    peers = st_count * tm_count * pol_count
    share = CH // peers
    inputs = row_count * st_count
    pol = lax.axis_index("pol")

    ending = lax.dynamic_slice(
        samples, (pol * ROWS, local_length - LEAD * NFFT), (ROWS, LEAD * NFFT)
    )
    halo = lax.ppermute(ending, "tm", [(i, i + 1) for i in range(tm_count - 1)])

    e, f = channel_order % FRAME_A, channel_order // FRAME_A
    row = jnp.minimum(e, FRAME_A - e) * (2 * LOW) + jnp.where(e > HALF_E, LOW, 0) + f
    rows = jnp.arange(CH + 2)
    here = jnp.where(rows == CH, pol, lax.axis_index("tm"))
    rows = jnp.where(rows < CH, jnp.pad(row * PER_SLOT, (0, 2)), here).astype(jnp.int32)
    cosine, sine = np_twist()
    consts = [jnp.asarray(c) for c in (np_window(), np_first(), cosine, sine, np_second())]

    parts = [5 * (share // 8), 3 * (share // 8)]
    groups = ROWS // GROUP
    late = filterbank(
        late_kernel, "filterbank_late", peers, [share], rows, [samples],
        [pl.BlockSpec((GROUP, local_length), lambda i, r: (r[CH] * groups + i, 0))],
        consts,
    )
    exchange = functools.partial(lax.all_to_all, axis_name=AXES, split_axis=0, concat_axis=0, tiled=True)
    late = exchange(late[0])
    early = filterbank(
        early_kernel, "filterbank_early", peers, parts, rows, [samples, halo, history],
        [
            pl.BlockSpec((GROUP, BATCH * NFFT), lambda i, r: (r[CH] * groups + i, 0)),
            pl.BlockSpec((GROUP, LEAD * NFFT), lambda i, r: (jnp.where(r[CH + 1] == 0, 0, i), 0)),
            pl.BlockSpec(
                (GROUP, LEAD * NFFT), lambda i, r: (jnp.where(r[CH + 1] == 0, r[CH] * groups + i, 0), 0)
            ),
        ],
        consts,
    )
    line = jnp.arange(inputs)
    target = 2 * jnp.repeat(station_order, 2) + line % 2
    keep = 1 - jnp.repeat(flagged, 2)
    perm = ((target[:, None] == line[None, :]) & (keep[None, :] == 1)).astype(jnp.bfloat16)

    early, rest, perm = lax.optimization_barrier((*early, perm))
    sizes = (st_count, tm_count, pol_count)
    early = exchange(early)
    late = order_late(share, sizes, late, perm)
    rest, late = lax.optimization_barrier((rest, late))
    rest = exchange(rest)

    scale = 1.0 / (spec_local * tm_count)
    common = (share, inputs, scale, sizes, late)
    out = correlate(0, parts[0], *common, early, perm, None)
    return correlate(parts[0], parts[1], *common, rest, perm, out)


def shifted(array, axis, by):
    peers = lax.axis_size(axis)
    pairs = [(i, i + by) for i in range(peers) if 0 <= i + by < peers]
    return lax.ppermute(array, axis, pairs)


def filter_window(tap_count, frame_size):
    length = tap_count * frame_size
    offsets = jnp.arange(length).astype(jnp.float32) + 0.5
    centred = (offsets - 0.5 * length) / frame_size
    tapering = 0.5 - 0.5 * jnp.cos(offsets * (2.0 * math.pi / length))
    return (jnp.sinc(centred) * tapering).reshape(tap_count, frame_size)


def polyphase(row_block, weights, spec_count):
    row_total = row_block.shape[0]
    tap_count, frame_size = weights.shape
    running = jnp.zeros((row_total, spec_count, frame_size), jnp.float32)
    for tap_index in range(tap_count):
        section = row_block[:, tap_index * frame_size : (tap_index + spec_count) * frame_size]
        section = section.reshape(row_total, spec_count, frame_size)
        running = running + section.astype(jnp.float32) * weights[tap_index]
    return running.astype(jnp.bfloat16).reshape(row_total * spec_count, frame_size)


def trig_pair(left, right, modulus, amplitude):
    turn_count = left[:, None] * right[None, :] % modulus
    angles = turn_count.astype(jnp.float32) * (2.0 * math.pi / modulus)
    cosine = (jnp.cos(angles) * amplitude).astype(jnp.bfloat16)
    sine_part = (-(jnp.sin(angles) * amplitude)).astype(jnp.bfloat16)
    return (cosine, sine_part)


def product_low(form, left, right):
    return jnp.einsum(form, left, right, preferred_element_type=jnp.float32)


def frame_transform(filtered, channels, first_len):
    row_total, frame_size = filtered.shape
    second_len = frame_size // first_len
    half_len = second_len // 2
    first_idx = jnp.arange(first_len)
    second_idx = jnp.arange(second_len)
    half_idx = jnp.arange(half_len)
    first_cos, first_sin = trig_pair(first_idx, first_idx, first_len, 1.0 / math.sqrt(first_len))
    blocks = filtered.reshape(row_total, first_len, second_len)
    segment_re = product_low("rab,ae->reb", blocks, first_cos)
    segment_im = product_low("rab,ae->reb", blocks, first_sin)
    twist_turns = first_idx[:, None] * second_idx[None, :] % frame_size
    twist_angles = twist_turns.astype(jnp.float32) * (2.0 * math.pi / frame_size)
    twist_cos = jnp.cos(twist_angles)
    twist_sin = jnp.sin(twist_angles)
    twist_re = (segment_re * twist_cos + segment_im * twist_sin).astype(jnp.bfloat16)
    twist_im = (segment_im * twist_cos - segment_re * twist_sin).astype(jnp.bfloat16)
    second_cos, second_sin = trig_pair(
        second_idx, half_idx, second_len, 1.0 / math.sqrt(second_len)
    )
    full_re = product_low("reb,bf->ref", twist_re, second_cos) - product_low(
        "reb,bf->ref", twist_im, second_sin
    )
    full_im = product_low("reb,bf->ref", twist_re, second_sin) + product_low(
        "reb,bf->ref", twist_im, second_cos
    )
    column = channels % first_len * half_len + channels // first_len
    flat_re = jnp.take(full_re.reshape(row_total, first_len * half_len), column, axis=1)
    flat_im = jnp.take(full_im.reshape(row_total, first_len * half_len), column, axis=1)
    return jnp.stack([flat_re, flat_im], axis=1)


def input_rows(station_order):
    station_total = station_order.shape[0]
    inverse = (
        jnp.zeros((station_total,), jnp.int32).at[station_order].set(jnp.arange(station_total))
    )
    polarity = jnp.tile(jnp.arange(2), station_total)
    return 2 * jnp.repeat(inverse, 2) + polarity


def packed_products(turned, norm_scale):
    input_count, spec_count, pair_count, slot_count = turned.shape
    arranged = turned.transpose(3, 0, 1, 2)
    stacked = arranged.reshape(slot_count, input_count, spec_count * 2)
    swapped = jnp.stack([-arranged[..., 1], arranged[..., 0]], axis=-1).reshape(
        slot_count, input_count, spec_count * 2
    )
    combined = jnp.concatenate([stacked, swapped], axis=1)
    visible = jnp.einsum("sik,sjk->sij", stacked, combined, preferred_element_type=jnp.float32)
    indices = jnp.arange(input_count)
    upper_half = indices[:, None] <= indices[None, :]
    return (
        jnp.where(upper_half[None], visible[:, :, :input_count], visible[:, :, input_count:])
        * norm_scale
    )


def general_body(samples, history, station_order, channel_order, flagged):
    row_count, local_length = samples.shape
    spec_local = local_length // NFFT
    st_count = lax.axis_size("st")
    tm_count = lax.axis_size("tm")
    pol_count = lax.axis_size("pol")
    slot_share = CH // (st_count * tm_count * pol_count)
    half_slots = CH // pol_count
    lead_length = (TAPS - 1) * NFFT
    earlier = shifted(samples[:, local_length - lead_length :], "tm", 1)
    earlier = jnp.where(lax.axis_index("tm") == 0, history, earlier)
    stream = jnp.concatenate([earlier, samples], axis=1)
    filtered = polyphase(stream, filter_window(TAPS, NFFT), spec_local)
    local_slots = jnp.arange(half_slots)
    global_slots = (
        local_slots // slot_share * (slot_share * pol_count)
        + lax.axis_index("pol") * slot_share
        + local_slots % slot_share
    )
    station_ids = lax.dynamic_slice_in_dim(
        station_order, lax.axis_index("st") * (row_count // 2), row_count // 2
    )
    keeping = jnp.repeat((1 - flagged[station_ids]).astype(jnp.float32), 2)
    product = frame_transform(filtered, channel_order[global_slots], FRAME_A)
    product = product.reshape(row_count, spec_local, 2, half_slots) * keeping[:, None, None, None]
    spectra = product.astype(jnp.bfloat16)
    norm_scale = 1.0 / (spec_local * tm_count)
    input_order = input_rows(station_order)
    turned = lax.all_to_all(
        lax.all_to_all(spectra, "st", split_axis=3, concat_axis=0, tiled=True),
        "tm",
        split_axis=3,
        concat_axis=1,
        tiled=True,
    )
    turned = jnp.take(turned, input_order, axis=0)
    return packed_products(turned, norm_scale)


def fits(samples, mesh):
    st_count, tm_count, pol_count = (mesh.shape[a] for a in AXES)
    rows = samples.shape[0] // st_count
    frames = samples.shape[1] // tm_count // NFFT
    share = CH // (st_count * tm_count * pol_count)
    return (
        rows == ROWS * pol_count
        and frames == 2 * BATCH
        and tm_count == 4
        and pol_count == 2
        and share % (8 * PREP) == 0
        and samples.shape[0] % 256 == 0
    )


def solution(mesh):
    def run(samples, history, station_order, channel_order, flagged):
        body = fused_body if fits(samples, mesh) else general_body
        return jax.shard_map(
            body,
            mesh=mesh,
            in_specs=(P("st", "tm"), P("st", None), P(), P(), P()),
            out_specs=P(("st", "tm", "pol"), None, None),
            check_vma=False,
        )(samples, history, station_order, channel_order, flagged)

    return run
```

```python
import functools
import math

import jax
import jax.numpy as jnp
import numpy as np
from jax import lax
from jax.experimental import pallas as pl
from jax.experimental.pallas import tpu as pltpu
from jax.sharding import PartitionSpec as P

NFFT = 8192
FRAME_A = 32
FRAME_B = NFFT // FRAME_A
CH = 2048
TAPS = 4
LEAD = TAPS - 1
HALF_E = FRAME_A // 2
LOW = CH // FRAME_A
AXES = ("st", "tm", "pol")
ROWS = 64
GROUP = 16
PREP = 8
BATCHED = 2
UNROLLED = 3
BATCH = 4
PAIRS = BATCH // 2
PER_SLOT = 2 * PAIRS
VMEM = 62 << 20
BANK_VMEM = 56 << 20


def np_window():
    length = TAPS * NFFT
    offsets = np.arange(length) + 0.5
    centred = (offsets - 0.5 * length) / NFFT
    tapering = 0.5 - 0.5 * np.cos(offsets * (2.0 * math.pi / length))
    return (np.sinc(centred) * tapering).reshape(TAPS, NFFT).astype(np.float32)


def np_first():
    turns = np.arange(FRAME_A)[:, None] * np.arange(FRAME_A)[None, :] % FRAME_A
    angles = turns * (2.0 * math.pi / FRAME_A)
    cosine = np.cos(angles) / math.sqrt(FRAME_A)
    sine = -np.sin(angles) / math.sqrt(FRAME_A)
    rows = [cosine[0], cosine[HALF_E]]
    for e in range(1, HALF_E):
        rows += [cosine[e], sine[e]]
    return np.kron(np.stack(rows), np.eye(GROUP)).astype(jnp.bfloat16)


def np_twist():
    turns = np.arange(HALF_E + 1)[:, None] * np.arange(FRAME_B)[None, :] % NFFT
    angles = turns * (2.0 * math.pi / NFFT)
    return np.cos(angles).astype(np.float32), np.sin(angles).astype(np.float32)


def np_second():
    f = np.concatenate([np.arange(LOW), FRAME_B - 1 - np.arange(LOW)])
    sign = np.where(np.arange(2 * LOW) < LOW, 1.0, -1.0)[:, None]
    angles = f[:, None] * np.arange(FRAME_B)[None, :] % FRAME_B * (2.0 * math.pi / FRAME_B)
    cosine = np.cos(angles) / math.sqrt(FRAME_B)
    sine = -np.sin(angles) / math.sqrt(FRAME_B)
    top = np.concatenate([cosine, -sine], axis=1)
    bottom = np.concatenate([sine * sign, cosine * sign], axis=1)
    return np.concatenate([top, bottom]).astype(jnp.bfloat16)


def filterbank_body(sources, step, refs):
    row_ref, w_ref, c1_ref, cos_ref, sin_ref, w2_ref, results, y_ref, t_ref, d_ref, sems, *outs = refs

    def filter_a(taps_of, a, carry):
        weights = [w_ref[k : k + 1, pl.ds(pl.multiple_of(a * FRAME_B, FRAME_B), FRAME_B)] for k in range(TAPS)]
        frames = [taps_of(i, a) for i in range(BATCH + LEAD)]
        for t in range(BATCH):
            total = frames[t] * weights[0]
            for k in range(1, TAPS):
                total = total + frames[t + k] * weights[k]
            y_ref[t, pl.ds(pl.multiple_of(a * GROUP, GROUP), GROUP), :] = total.astype(jnp.bfloat16)
        return carry

    if len(sources) == 1:
        lax.fori_loop(0, FRAME_A, functools.partial(filter_a, sources[0]), 0, unroll=2)
    else:
        opening = row_ref[CH + 1] == 0

        @pl.when(opening)
        def _():
            lax.fori_loop(0, FRAME_A, functools.partial(filter_a, sources[0]), 0, unroll=2)

        @pl.when(jnp.logical_not(opening))
        def _():
            lax.fori_loop(0, FRAME_A, functools.partial(filter_a, sources[1]), 0, unroll=2)

    def first_t(t, carry):
        seg = jnp.dot(c1_ref[...], y_ref[t], preferred_element_type=jnp.float32)
        rows = pl.ds(pl.multiple_of(t * ROWS + step * GROUP, GROUP), GROUP)
        for e in range(HALF_E + 1):
            cosine = cos_ref[e : e + 1, :]
            sine = sin_ref[e : e + 1, :]
            if e == 0 or e == HALF_E:
                at = 0 if e == 0 else GROUP
                re = seg[at : at + GROUP]
                twist_re = re * cosine
                twist_im = -(re * sine)
            else:
                at = 2 * e * GROUP
                re = seg[at : at + GROUP]
                im = seg[at + GROUP : at + 2 * GROUP]
                twist_re = re * cosine + im * sine
                twist_im = im * cosine - re * sine
            t_ref[e, rows, 0:FRAME_B] = twist_re.astype(jnp.bfloat16)
            t_ref[e, rows, FRAME_B : 2 * FRAME_B] = twist_im.astype(jnp.bfloat16)
        return carry

    lax.fori_loop(0, BATCH, first_t, 0, unroll=True)

    @pl.when(step == ROWS // GROUP - 1)
    def _():
        for e in range(HALF_E + 1):
            full = lax.dot_general(
                w2_ref[...], t_ref[e], (((1,), (1,)), ((), ())), preferred_element_type=jnp.float32
            )
            for c in range(2):
                for pair in range(PAIRS):
                    start = PER_SLOT + e * 2 * LOW * PER_SLOT + c * PAIRS + pair
                    d_ref[pl.ds(start, 2 * LOW, stride=PER_SLOT), :] = full[
                        c * 2 * LOW : (c + 1) * 2 * LOW, pair * 128 : (pair + 1) * 128
                    ]

        share = sum(out_ref.shape[1] for out_ref in outs) // PER_SLOT
        lower = lax.broadcasted_iota(jnp.int32, (2 * PER_SLOT, 128), 0) < PER_SLOT

        def gather(peer, carry):
            slot = peer * share
            for out_ref in outs:
                for at in range(0, out_ref.shape[1], 4 * PER_SLOT):
                    halves = []
                    for k in (0, 2):
                        one = d_ref[pl.ds(row_ref[slot + k] + PER_SLOT, 2 * PER_SLOT), :]
                        two = d_ref[pl.ds(row_ref[slot + k + 1], 2 * PER_SLOT), :]
                        halves.append(jnp.where(lower, one, two))
                    slot = slot + 4
                    out_ref[peer, at : at + 4 * PER_SLOT, :] = jnp.concatenate(halves).astype(jnp.bfloat16)
            return carry

        quarter = outs[0].shape[0] // 4
        copies = []
        for q in range(4):
            lax.fori_loop(q * quarter, (q + 1) * quarter, gather, 0)
            for n, (out_ref, result_ref) in enumerate(zip(outs, results)):
                peers = pl.ds(q * quarter, quarter)
                copies.append(
                    pltpu.make_async_copy(out_ref.at[peers], result_ref.at[peers], sems.at[n, q])
                )
                copies[-1].start()
        for copy in copies:
            copy.wait()


def late_kernel(row_ref, x_ref, w_ref, c1_ref, cos_ref, sin_ref, w2_ref, *rest):
    count = (len(rest) - 4) // 2
    results, scratch = rest[:count], rest[count:]

    def taps_of(i, a):
        at = pl.multiple_of(i * NFFT + a * FRAME_B, FRAME_B)
        return x_ref[:, pl.ds(at, FRAME_B)].astype(jnp.float32)

    refs = (row_ref, w_ref, c1_ref, cos_ref, sin_ref, w2_ref, results, *scratch)
    filterbank_body([taps_of], pl.program_id(0), refs)


def early_kernel(
    row_ref, x_ref, halo_ref, history_ref, w_ref, c1_ref, cos_ref, sin_ref, w2_ref, *rest
):
    count = (len(rest) - 4) // 2
    results, scratch = rest[:count], rest[count:]

    def taps_from(ahead_ref):
        def taps_of(i, a):
            source, at = (x_ref, i - LEAD) if i >= LEAD else (ahead_ref, i)
            at = pl.multiple_of(at * NFFT + a * FRAME_B, FRAME_B)
            return source[:, pl.ds(at, FRAME_B)].astype(jnp.float32)

        return taps_of

    refs = (row_ref, w_ref, c1_ref, cos_ref, sin_ref, w2_ref, results, *scratch)
    filterbank_body([taps_from(history_ref), taps_from(halo_ref)], pl.program_id(0), refs)


def filterbank(kernel, name, peers, parts, rows, streams, stream_specs, consts):
    whole = [pl.BlockSpec(c.shape, lambda i, r: (0, 0)) for c in consts]
    outs = [jax.ShapeDtypeStruct((peers, part * PER_SLOT, 128), jnp.bfloat16) for part in parts]
    return pl.pallas_call(
        kernel,
        out_shape=outs,
        grid_spec=pltpu.PrefetchScalarGridSpec(
            num_scalar_prefetch=1,
            grid=(ROWS // GROUP,),
            in_specs=stream_specs + whole,
            out_specs=[pl.BlockSpec(memory_space=pl.ANY)] * len(outs),
            scratch_shapes=[
                pltpu.VMEM((BATCH, FRAME_A * GROUP, FRAME_B), jnp.bfloat16),
                pltpu.VMEM((HALF_E + 1, BATCH * ROWS, 2 * FRAME_B), jnp.bfloat16),
                pltpu.VMEM(((HALF_E + 1) * 2 * LOW * PER_SLOT + 2 * PER_SLOT, 128), jnp.float32),
                pltpu.SemaphoreType.DMA((len(outs), 4)),
                *[pltpu.VMEM(out.shape, out.dtype) for out in outs],
            ],
        ),
        cost_estimate=pl.CostEstimate(flops=12 * 10**9, bytes_accessed=16 << 20, transcendentals=0),
        compiler_params=pltpu.CompilerParams(
            dimension_semantics=("arbitrary",), vmem_limit_bytes=BANK_VMEM
        ),
        name=name,
    )(rows, *streams, *consts)


def order_inputs(source, perm_ref, lhs_ref, z_ref, sizes, span):
    st_count, tm_count, pol_count = sizes
    half = 128 // 2
    for tm in range(tm_count):
        for st in range(st_count):
            blocks = [source[(st * tm_count + tm) * pol_count + pol] for pol in range(pol_count)]
            lanes = slice(st * pol_count * half, (st + 1) * pol_count * half)
            for odd in range(2):
                row = (odd * tm_count + tm) * span
                lhs_ref[row : row + span, lanes] = jnp.concatenate(
                    [block[:, odd * half : (odd + 1) * half] for block in blocks], axis=1
                )
    turned = jnp.dot(lhs_ref[...], perm_ref[...], preferred_element_type=jnp.float32)
    for j in range(z_ref.shape[0]):
        z_ref[j, : turned.shape[0]] = turned[:, j * 128 : (j + 1) * 128]


def slot_rows(z_ref, slot, c, span, count):
    tiles = [
        jnp.concatenate(
            [
                z_ref[j, pl.ds(slot * PER_SLOT + c * PAIRS + pair, count, stride=span), :]
                for j in range(z_ref.shape[0])
            ],
            axis=1,
        )
        for pair in range(PAIRS)
    ]
    return jnp.concatenate(tiles, axis=0).astype(jnp.bfloat16)


def order_kernel(sizes, late_ref, perm_ref, out_ref, lhs_ref, z_ref):
    slots = out_ref.shape[0]
    span = slots * PER_SLOT
    order_inputs(late_ref, perm_ref, lhs_ref, z_ref, sizes, span)
    count = 2 * sizes[1]
    for slot in range(slots):
        for c in range(2):
            out_ref[slot, c * PAIRS * count : (c + 1) * PAIRS * count, :] = slot_rows(
                z_ref, slot, c, span, count
            )


def order_late(part, sizes, late, perm):
    peers = late.shape[0]
    inputs = perm.shape[1]
    span = PREP * PER_SLOT
    rows = 2 * sizes[1] * span
    depth = 2 * sizes[1] * PER_SLOT
    return pl.pallas_call(
        functools.partial(order_kernel, sizes),
        out_shape=jax.ShapeDtypeStruct((part, depth, inputs), jnp.bfloat16),
        grid=(part // PREP,),
        in_specs=[
            pl.BlockSpec((peers, span, 128), lambda i: (0, i, 0)),
            pl.BlockSpec(perm.shape, lambda i: (0, 0)),
        ],
        out_specs=pl.BlockSpec((PREP, depth, inputs), lambda i: (i, 0, 0)),
        scratch_shapes=[
            pltpu.VMEM((rows, inputs), jnp.bfloat16),
            pltpu.VMEM((inputs // 128, rows + PREP * PER_SLOT, 128), jnp.float32),
        ],
        cost_estimate=pl.CostEstimate(flops=8 * 10**9, bytes_accessed=4 << 20, transcendentals=0),
        compiler_params=pltpu.CompilerParams(
            dimension_semantics=("arbitrary",), vmem_limit_bytes=VMEM
        ),
        name="order_late",
    )(late, perm)


def correlate_kernel(scale, sizes, start, *refs):
    late_ref, arrived_ref, perm_ref = refs[:3]
    out_ref, lhs_ref, z_ref, ordered_ref, buffer_ref, sems = refs[-6:]
    inputs = perm_ref.shape[1]
    span = PREP * PER_SLOT
    count = 2 * sizes[1]
    depth = PAIRS * count
    batches, batch = buffer_ref.shape[:2]
    tile = 128
    tall = lax.broadcasted_iota(jnp.int32, (tile, tile), 0)
    wide = lax.broadcasted_iota(jnp.int32, (tile, tile), 1)
    upper = tall <= wide

    def leave(group, k):
        first = start + group * PREP + k * batch
        return pltpu.make_async_copy(
            buffer_ref.at[k], out_ref.at[pl.ds(first, batch)], sems.at[k]
        )

    def products(z, turned, left, into):
        for at in range(0, inputs, tile):
            rows = slice(at, at + tile)
            sides = jnp.concatenate([turned[:, : at + tile], z[:, at:]], axis=1)
            both = jnp.dot(left[rows], sides, preferred_element_type=jnp.float32) * scale
            if at > 0:
                into[rows, :at] = both[:, :at]
            into[rows, rows] = jnp.where(
                upper, both[:, at + tile : at + 2 * tile], both[:, at : at + tile]
            )
            if at + tile < inputs:
                into[rows, at + tile :] = both[:, at + 2 * tile :]

    def order(group, parity):
        source = arrived_ref.at[:, pl.ds(pl.multiple_of(group * span, span), span), :]
        order_inputs(source, perm_ref, lhs_ref, z_ref, sizes, span)
        for slot in range(PREP):
            for c in range(2):
                ordered_ref[parity, slot, c * depth : (c + 1) * depth, :] = slot_rows(
                    z_ref, slot, c, span, count
                )

    groups = late_ref.shape[0] // PREP

    def work(group, parity, fresh, following):
        for k in range(batches):
            if not fresh:
                leave(group - 1, k).wait()
            if k == 1 and following is not None:
                order(following, 1 - parity)
            for i in range(batch):
                slot = k * batch + i
                z = jnp.concatenate([ordered_ref[parity, slot], late_ref[group * PREP + slot]], axis=0)
                turned = []
                for at in range(0, z.shape[0], 2 * depth):
                    turned += [-z[at + depth : at + 2 * depth], z[at : at + depth]]
                turned = jnp.concatenate(turned, axis=0)
                products(z, turned, z.T, buffer_ref.at[k, i])
            leave(group, k).start()

    order(0, 0)
    if groups <= UNROLLED:
        for group in range(groups):
            work(group, group % 2, group == 0, group + 1 if group + 1 < groups else None)
    else:

        def follow(group, carry):
            work(group, lax.rem(group, 2), False, jnp.minimum(group + 1, groups - 1))
            return carry

        work(0, 0, True, 1)
        lax.fori_loop(1, groups, follow, 0)
    for k in range(batches):
        leave(groups - 1, k).wait()


def correlate(start, part, share, inputs, scale, sizes, late, arrived, perm, before):
    depth = late.shape[1]
    rows = 2 * sizes[1] * PREP * PER_SLOT
    operands = [late, arrived, perm]
    in_specs = [
        pl.BlockSpec((pl.Element(part), pl.Element(depth), pl.Element(inputs)), lambda i: (start, 0, 0)),
        pl.BlockSpec(arrived.shape, lambda i: (0, 0, 0)),
        pl.BlockSpec(perm.shape, lambda i: (0, 0)),
    ]
    aliases = {}
    if before is not None:
        in_specs.append(pl.BlockSpec(memory_space=pl.ANY))
        aliases = {len(operands): 0}
        operands.append(before)
    return pl.pallas_call(
        functools.partial(correlate_kernel, scale, sizes, start),
        out_shape=jax.ShapeDtypeStruct((share, inputs, inputs), jnp.float32),
        grid=(1,),
        in_specs=in_specs,
        out_specs=pl.BlockSpec(memory_space=pl.ANY),
        scratch_shapes=[
            pltpu.VMEM((rows, inputs), jnp.bfloat16),
            pltpu.VMEM((inputs // 128, rows + PREP * PER_SLOT, 128), jnp.float32),
            pltpu.VMEM((2, PREP, depth, inputs), jnp.bfloat16),
            pltpu.VMEM((PREP // BATCHED, BATCHED, inputs, inputs), jnp.float32),
            pltpu.SemaphoreType.DMA((PREP // BATCHED,)),
        ],
        input_output_aliases=aliases,
        cost_estimate=pl.CostEstimate(
            flops=part * 12 * 10**7, bytes_accessed=part * inputs * inputs * 4, transcendentals=0
        ),
        compiler_params=pltpu.CompilerParams(
            dimension_semantics=("arbitrary",), vmem_limit_bytes=VMEM
        ),
        name="correlate",
    )(*operands)


def fused_body(samples, history, station_order, channel_order, flagged):
    row_count, local_length = samples.shape
    spec_local = local_length // NFFT
    st_count = lax.axis_size("st")
    tm_count = lax.axis_size("tm")
    pol_count = lax.axis_size("pol")
    peers = st_count * tm_count * pol_count
    share = CH // peers
    inputs = row_count * st_count
    pol = lax.axis_index("pol")

    ending = lax.dynamic_slice(
        samples, (pol * ROWS, local_length - LEAD * NFFT), (ROWS, LEAD * NFFT)
    )
    halo = lax.ppermute(ending, "tm", [(i, i + 1) for i in range(tm_count - 1)])

    e, f = channel_order % FRAME_A, channel_order // FRAME_A
    row = jnp.minimum(e, FRAME_A - e) * (2 * LOW) + jnp.where(e > HALF_E, LOW, 0) + f
    rows = jnp.arange(CH + 2)
    here = jnp.where(rows == CH, pol, lax.axis_index("tm"))
    rows = jnp.where(rows < CH, jnp.pad(row * PER_SLOT, (0, 2)), here).astype(jnp.int32)
    cosine, sine = np_twist()
    consts = [jnp.asarray(c) for c in (np_window(), np_first(), cosine, sine, np_second())]

    parts = [5 * (share // 8), 3 * (share // 8)]
    groups = ROWS // GROUP
    late = filterbank(
        late_kernel, "filterbank_late", peers, [share], rows, [samples],
        [
            pl.BlockSpec(
                (pl.Element(GROUP), pl.Element((BATCH + LEAD) * NFFT)),
                lambda i, r: ((r[CH] * groups + i) * GROUP, local_length - (BATCH + LEAD) * NFFT),
            )
        ],
        consts,
    )
    exchange = functools.partial(lax.all_to_all, axis_name=AXES, split_axis=0, concat_axis=0, tiled=True)
    late = exchange(late[0])
    early = filterbank(
        early_kernel, "filterbank_early", peers, parts, rows, [samples, halo, history],
        [
            pl.BlockSpec((GROUP, BATCH * NFFT), lambda i, r: (r[CH] * groups + i, 0)),
            pl.BlockSpec((GROUP, LEAD * NFFT), lambda i, r: (jnp.where(r[CH + 1] == 0, 0, i), 0)),
            pl.BlockSpec(
                (GROUP, LEAD * NFFT), lambda i, r: (jnp.where(r[CH + 1] == 0, r[CH] * groups + i, 0), 0)
            ),
        ],
        consts,
    )
    line = jnp.arange(inputs)
    target = 2 * jnp.repeat(station_order, 2) + line % 2
    keep = 1 - jnp.repeat(flagged, 2)
    perm = ((target[:, None] == line[None, :]) & (keep[None, :] == 1)).astype(jnp.bfloat16)

    early, rest, perm = lax.optimization_barrier((*early, perm))
    sizes = (st_count, tm_count, pol_count)
    early = exchange(early)
    late = order_late(share, sizes, late, perm)
    rest, late = lax.optimization_barrier((rest, late))
    rest = exchange(rest)

    scale = 1.0 / (spec_local * tm_count)
    common = (share, inputs, scale, sizes, late)
    out = correlate(0, parts[0], *common, early, perm, None)
    return correlate(parts[0], parts[1], *common, rest, perm, out)


def shifted(array, axis, by):
    peers = lax.axis_size(axis)
    pairs = [(i, i + by) for i in range(peers) if 0 <= i + by < peers]
    return lax.ppermute(array, axis, pairs)


def filter_window(tap_count, frame_size):
    length = tap_count * frame_size
    offsets = jnp.arange(length).astype(jnp.float32) + 0.5
    centred = (offsets - 0.5 * length) / frame_size
    tapering = 0.5 - 0.5 * jnp.cos(offsets * (2.0 * math.pi / length))
    return (jnp.sinc(centred) * tapering).reshape(tap_count, frame_size)


def polyphase(row_block, weights, spec_count):
    row_total = row_block.shape[0]
    tap_count, frame_size = weights.shape
    running = jnp.zeros((row_total, spec_count, frame_size), jnp.float32)
    for tap_index in range(tap_count):
        section = row_block[:, tap_index * frame_size : (tap_index + spec_count) * frame_size]
        section = section.reshape(row_total, spec_count, frame_size)
        running = running + section.astype(jnp.float32) * weights[tap_index]
    return running.astype(jnp.bfloat16).reshape(row_total * spec_count, frame_size)


def trig_pair(left, right, modulus, amplitude):
    turn_count = left[:, None] * right[None, :] % modulus
    angles = turn_count.astype(jnp.float32) * (2.0 * math.pi / modulus)
    cosine = (jnp.cos(angles) * amplitude).astype(jnp.bfloat16)
    sine_part = (-(jnp.sin(angles) * amplitude)).astype(jnp.bfloat16)
    return (cosine, sine_part)


def product_low(form, left, right):
    return jnp.einsum(form, left, right, preferred_element_type=jnp.float32)


def frame_transform(filtered, channels, first_len):
    row_total, frame_size = filtered.shape
    second_len = frame_size // first_len
    half_len = second_len // 2
    first_idx = jnp.arange(first_len)
    second_idx = jnp.arange(second_len)
    half_idx = jnp.arange(half_len)
    first_cos, first_sin = trig_pair(first_idx, first_idx, first_len, 1.0 / math.sqrt(first_len))
    blocks = filtered.reshape(row_total, first_len, second_len)
    segment_re = product_low("rab,ae->reb", blocks, first_cos)
    segment_im = product_low("rab,ae->reb", blocks, first_sin)
    twist_turns = first_idx[:, None] * second_idx[None, :] % frame_size
    twist_angles = twist_turns.astype(jnp.float32) * (2.0 * math.pi / frame_size)
    twist_cos = jnp.cos(twist_angles)
    twist_sin = jnp.sin(twist_angles)
    twist_re = (segment_re * twist_cos + segment_im * twist_sin).astype(jnp.bfloat16)
    twist_im = (segment_im * twist_cos - segment_re * twist_sin).astype(jnp.bfloat16)
    second_cos, second_sin = trig_pair(
        second_idx, half_idx, second_len, 1.0 / math.sqrt(second_len)
    )
    full_re = product_low("reb,bf->ref", twist_re, second_cos) - product_low(
        "reb,bf->ref", twist_im, second_sin
    )
    full_im = product_low("reb,bf->ref", twist_re, second_sin) + product_low(
        "reb,bf->ref", twist_im, second_cos
    )
    column = channels % first_len * half_len + channels // first_len
    flat_re = jnp.take(full_re.reshape(row_total, first_len * half_len), column, axis=1)
    flat_im = jnp.take(full_im.reshape(row_total, first_len * half_len), column, axis=1)
    return jnp.stack([flat_re, flat_im], axis=1)


def input_rows(station_order):
    station_total = station_order.shape[0]
    inverse = (
        jnp.zeros((station_total,), jnp.int32).at[station_order].set(jnp.arange(station_total))
    )
    polarity = jnp.tile(jnp.arange(2), station_total)
    return 2 * jnp.repeat(inverse, 2) + polarity


def packed_products(turned, norm_scale):
    input_count, spec_count, pair_count, slot_count = turned.shape
    arranged = turned.transpose(3, 0, 1, 2)
    stacked = arranged.reshape(slot_count, input_count, spec_count * 2)
    swapped = jnp.stack([-arranged[..., 1], arranged[..., 0]], axis=-1).reshape(
        slot_count, input_count, spec_count * 2
    )
    combined = jnp.concatenate([stacked, swapped], axis=1)
    visible = jnp.einsum("sik,sjk->sij", stacked, combined, preferred_element_type=jnp.float32)
    indices = jnp.arange(input_count)
    upper_half = indices[:, None] <= indices[None, :]
    return (
        jnp.where(upper_half[None], visible[:, :, :input_count], visible[:, :, input_count:])
        * norm_scale
    )


def general_body(samples, history, station_order, channel_order, flagged):
    row_count, local_length = samples.shape
    spec_local = local_length // NFFT
    st_count = lax.axis_size("st")
    tm_count = lax.axis_size("tm")
    pol_count = lax.axis_size("pol")
    slot_share = CH // (st_count * tm_count * pol_count)
    half_slots = CH // pol_count
    lead_length = (TAPS - 1) * NFFT
    earlier = shifted(samples[:, local_length - lead_length :], "tm", 1)
    earlier = jnp.where(lax.axis_index("tm") == 0, history, earlier)
    stream = jnp.concatenate([earlier, samples], axis=1)
    filtered = polyphase(stream, filter_window(TAPS, NFFT), spec_local)
    local_slots = jnp.arange(half_slots)
    global_slots = (
        local_slots // slot_share * (slot_share * pol_count)
        + lax.axis_index("pol") * slot_share
        + local_slots % slot_share
    )
    station_ids = lax.dynamic_slice_in_dim(
        station_order, lax.axis_index("st") * (row_count // 2), row_count // 2
    )
    keeping = jnp.repeat((1 - flagged[station_ids]).astype(jnp.float32), 2)
    product = frame_transform(filtered, channel_order[global_slots], FRAME_A)
    product = product.reshape(row_count, spec_local, 2, half_slots) * keeping[:, None, None, None]
    spectra = product.astype(jnp.bfloat16)
    norm_scale = 1.0 / (spec_local * tm_count)
    input_order = input_rows(station_order)
    turned = lax.all_to_all(
        lax.all_to_all(spectra, "st", split_axis=3, concat_axis=0, tiled=True),
        "tm",
        split_axis=3,
        concat_axis=1,
        tiled=True,
    )
    turned = jnp.take(turned, input_order, axis=0)
    return packed_products(turned, norm_scale)


def fits(samples, mesh):
    st_count, tm_count, pol_count = (mesh.shape[a] for a in AXES)
    rows = samples.shape[0] // st_count
    frames = samples.shape[1] // tm_count // NFFT
    share = CH // (st_count * tm_count * pol_count)
    return (
        rows == ROWS * pol_count
        and frames == 2 * BATCH
        and tm_count == 4
        and pol_count == 2
        and share % (8 * PREP) == 0
        and samples.shape[0] % 256 == 0
    )


def solution(mesh):
    def run(samples, history, station_order, channel_order, flagged):
        body = fused_body if fits(samples, mesh) else general_body
        return jax.shard_map(
            body,
            mesh=mesh,
            in_specs=(P("st", "tm"), P("st", None), P(), P(), P()),
            out_specs=P(("st", "tm", "pol"), None, None),
            check_vma=False,
        )(samples, history, station_order, channel_order, flagged)

    return run
```

```python
import functools
import math

import jax
import jax.numpy as jnp
import numpy as np
from jax import lax
from jax.experimental import pallas as pl
from jax.experimental.pallas import tpu as pltpu
from jax.sharding import PartitionSpec as P

NFFT = 8192
FRAME_A = 32
FRAME_B = NFFT // FRAME_A
CH = 2048
TAPS = 4
LEAD = TAPS - 1
HALF_E = FRAME_A // 2
LOW = CH // FRAME_A
AXES = ("st", "tm", "pol")
ROWS = 64
GROUP = 16
PREP = 8
BATCHED = 2
UNROLLED = 3
BATCH = 4
PAIRS = BATCH // 2
PER_SLOT = 2 * PAIRS
VMEM = 62 << 20
BANK_VMEM = 56 << 20


def np_window():
    length = TAPS * NFFT
    offsets = np.arange(length) + 0.5
    centred = (offsets - 0.5 * length) / NFFT
    tapering = 0.5 - 0.5 * np.cos(offsets * (2.0 * math.pi / length))
    return (np.sinc(centred) * tapering).reshape(TAPS, NFFT).astype(np.float32)


def np_first():
    turns = np.arange(FRAME_A)[:, None] * np.arange(FRAME_A)[None, :] % FRAME_A
    angles = turns * (2.0 * math.pi / FRAME_A)
    cosine = np.cos(angles) / math.sqrt(FRAME_A)
    sine = -np.sin(angles) / math.sqrt(FRAME_A)
    rows = [cosine[0], cosine[HALF_E]]
    for e in range(1, HALF_E):
        rows += [cosine[e], sine[e]]
    return np.kron(np.stack(rows), np.eye(GROUP)).astype(jnp.bfloat16)


def np_twist():
    turns = np.arange(HALF_E + 1)[:, None] * np.arange(FRAME_B)[None, :] % NFFT
    angles = turns * (2.0 * math.pi / NFFT)
    return np.cos(angles).astype(np.float32), np.sin(angles).astype(np.float32)


def np_second():
    f = np.concatenate([np.arange(LOW), FRAME_B - 1 - np.arange(LOW)])
    sign = np.where(np.arange(2 * LOW) < LOW, 1.0, -1.0)[:, None]
    angles = f[:, None] * np.arange(FRAME_B)[None, :] % FRAME_B * (2.0 * math.pi / FRAME_B)
    cosine = np.cos(angles) / math.sqrt(FRAME_B)
    sine = -np.sin(angles) / math.sqrt(FRAME_B)
    top = np.concatenate([cosine, -sine], axis=1)
    bottom = np.concatenate([sine * sign, cosine * sign], axis=1)
    return np.concatenate([top, bottom]).astype(jnp.bfloat16)


def filterbank_body(sources, step, refs):
    row_ref, w_ref, c1_ref, cos_ref, sin_ref, w2_ref, results, y_ref, t_ref, d_ref, sems, *outs = refs

    def filter_a(taps_of, a, carry):
        at = pl.multiple_of(a * FRAME_B, FRAME_B)
        weights = [w_ref[k : k + 1, pl.ds(at, FRAME_B)].astype(jnp.bfloat16) for k in range(TAPS)]
        frames = [taps_of(i, a) for i in range(BATCH + LEAD)]
        for t in range(BATCH):
            total = frames[t] * weights[0]
            for k in range(1, TAPS):
                total = total + frames[t + k] * weights[k]
            y_ref[t, pl.ds(pl.multiple_of(a * GROUP, GROUP), GROUP), :] = total
        return carry

    if len(sources) == 1:
        lax.fori_loop(0, FRAME_A, functools.partial(filter_a, sources[0]), 0, unroll=2)
    else:
        opening = row_ref[CH + 1] == 0

        @pl.when(opening)
        def _():
            lax.fori_loop(0, FRAME_A, functools.partial(filter_a, sources[0]), 0, unroll=2)

        @pl.when(jnp.logical_not(opening))
        def _():
            lax.fori_loop(0, FRAME_A, functools.partial(filter_a, sources[1]), 0, unroll=2)

    def first_t(t, carry):
        seg = jnp.dot(c1_ref[...], y_ref[t], preferred_element_type=jnp.float32)
        rows = pl.ds(pl.multiple_of(t * ROWS + step * GROUP, GROUP), GROUP)
        for e in range(HALF_E + 1):
            cosine = cos_ref[e : e + 1, :]
            sine = sin_ref[e : e + 1, :]
            if e == 0 or e == HALF_E:
                at = 0 if e == 0 else GROUP
                re = seg[at : at + GROUP]
                twist_re = re * cosine
                twist_im = -(re * sine)
            else:
                at = 2 * e * GROUP
                re = seg[at : at + GROUP]
                im = seg[at + GROUP : at + 2 * GROUP]
                twist_re = re * cosine + im * sine
                twist_im = im * cosine - re * sine
            t_ref[e, rows, 0:FRAME_B] = twist_re.astype(jnp.bfloat16)
            t_ref[e, rows, FRAME_B : 2 * FRAME_B] = twist_im.astype(jnp.bfloat16)
        return carry

    lax.fori_loop(0, BATCH, first_t, 0, unroll=True)

    @pl.when(step == ROWS // GROUP - 1)
    def _():
        for e in range(HALF_E + 1):
            full = lax.dot_general(
                w2_ref[...], t_ref[e], (((1,), (1,)), ((), ())), preferred_element_type=jnp.float32
            )
            for c in range(2):
                for pair in range(PAIRS):
                    start = PER_SLOT + e * 2 * LOW * PER_SLOT + c * PAIRS + pair
                    d_ref[pl.ds(start, 2 * LOW, stride=PER_SLOT), :] = full[
                        c * 2 * LOW : (c + 1) * 2 * LOW, pair * 128 : (pair + 1) * 128
                    ]

        share = sum(out_ref.shape[1] for out_ref in outs) // PER_SLOT
        lower = lax.broadcasted_iota(jnp.int32, (2 * PER_SLOT, 128), 0) < PER_SLOT

        def gather(peer, carry):
            slot = peer * share
            for out_ref in outs:
                for at in range(0, out_ref.shape[1], 4 * PER_SLOT):
                    halves = []
                    for k in (0, 2):
                        one = d_ref[pl.ds(row_ref[slot + k] + PER_SLOT, 2 * PER_SLOT), :]
                        two = d_ref[pl.ds(row_ref[slot + k + 1], 2 * PER_SLOT), :]
                        halves.append(jnp.where(lower, one, two))
                    slot = slot + 4
                    out_ref[peer, at : at + 4 * PER_SLOT, :] = jnp.concatenate(halves).astype(jnp.bfloat16)
            return carry

        quarter = outs[0].shape[0] // 4
        copies = []
        for q in range(4):
            lax.fori_loop(q * quarter, (q + 1) * quarter, gather, 0)
            for n, (out_ref, result_ref) in enumerate(zip(outs, results)):
                peers = pl.ds(q * quarter, quarter)
                copies.append(
                    pltpu.make_async_copy(out_ref.at[peers], result_ref.at[peers], sems.at[n, q])
                )
                copies[-1].start()
        for copy in copies:
            copy.wait()


def late_kernel(row_ref, x_ref, w_ref, c1_ref, cos_ref, sin_ref, w2_ref, *rest):
    count = (len(rest) - 4) // 2
    results, scratch = rest[:count], rest[count:]

    def taps_of(i, a):
        at = pl.multiple_of(i * NFFT + a * FRAME_B, FRAME_B)
        return x_ref[:, pl.ds(at, FRAME_B)]

    refs = (row_ref, w_ref, c1_ref, cos_ref, sin_ref, w2_ref, results, *scratch)
    filterbank_body([taps_of], pl.program_id(0), refs)


def early_kernel(
    row_ref, x_ref, halo_ref, history_ref, w_ref, c1_ref, cos_ref, sin_ref, w2_ref, *rest
):
    count = (len(rest) - 4) // 2
    results, scratch = rest[:count], rest[count:]

    def taps_from(ahead_ref):
        def taps_of(i, a):
            source, at = (x_ref, i - LEAD) if i >= LEAD else (ahead_ref, i)
            at = pl.multiple_of(at * NFFT + a * FRAME_B, FRAME_B)
            return source[:, pl.ds(at, FRAME_B)]

        return taps_of

    refs = (row_ref, w_ref, c1_ref, cos_ref, sin_ref, w2_ref, results, *scratch)
    filterbank_body([taps_from(history_ref), taps_from(halo_ref)], pl.program_id(0), refs)


def filterbank(kernel, name, peers, parts, rows, streams, stream_specs, consts):
    whole = [pl.BlockSpec(c.shape, lambda i, r: (0, 0)) for c in consts]
    outs = [jax.ShapeDtypeStruct((peers, part * PER_SLOT, 128), jnp.bfloat16) for part in parts]
    return pl.pallas_call(
        kernel,
        out_shape=outs,
        grid_spec=pltpu.PrefetchScalarGridSpec(
            num_scalar_prefetch=1,
            grid=(ROWS // GROUP,),
            in_specs=stream_specs + whole,
            out_specs=[pl.BlockSpec(memory_space=pl.ANY)] * len(outs),
            scratch_shapes=[
                pltpu.VMEM((BATCH, FRAME_A * GROUP, FRAME_B), jnp.bfloat16),
                pltpu.VMEM((HALF_E + 1, BATCH * ROWS, 2 * FRAME_B), jnp.bfloat16),
                pltpu.VMEM(((HALF_E + 1) * 2 * LOW * PER_SLOT + 2 * PER_SLOT, 128), jnp.float32),
                pltpu.SemaphoreType.DMA((len(outs), 4)),
                *[pltpu.VMEM(out.shape, out.dtype) for out in outs],
            ],
        ),
        cost_estimate=pl.CostEstimate(flops=12 * 10**9, bytes_accessed=16 << 20, transcendentals=0),
        compiler_params=pltpu.CompilerParams(
            dimension_semantics=("arbitrary",), vmem_limit_bytes=BANK_VMEM
        ),
        name=name,
    )(rows, *streams, *consts)


def order_inputs(source, perm_ref, lhs_ref, z_ref, sizes, span):
    st_count, tm_count, pol_count = sizes
    half = 128 // 2
    for tm in range(tm_count):
        for st in range(st_count):
            blocks = [source[(st * tm_count + tm) * pol_count + pol] for pol in range(pol_count)]
            lanes = slice(st * pol_count * half, (st + 1) * pol_count * half)
            for odd in range(2):
                row = (odd * tm_count + tm) * span
                lhs_ref[row : row + span, lanes] = jnp.concatenate(
                    [block[:, odd * half : (odd + 1) * half] for block in blocks], axis=1
                )
    turned = jnp.dot(lhs_ref[...], perm_ref[...], preferred_element_type=jnp.float32)
    for j in range(z_ref.shape[0]):
        z_ref[j, : turned.shape[0]] = turned[:, j * 128 : (j + 1) * 128]


def slot_rows(z_ref, slot, c, span, count):
    tiles = [
        jnp.concatenate(
            [
                z_ref[j, pl.ds(slot * PER_SLOT + c * PAIRS + pair, count, stride=span), :]
                for j in range(z_ref.shape[0])
            ],
            axis=1,
        )
        for pair in range(PAIRS)
    ]
    return jnp.concatenate(tiles, axis=0).astype(jnp.bfloat16)


def order_kernel(sizes, late_ref, perm_ref, out_ref, lhs_ref, z_ref):
    slots = out_ref.shape[0]
    span = slots * PER_SLOT
    order_inputs(late_ref, perm_ref, lhs_ref, z_ref, sizes, span)
    count = 2 * sizes[1]
    for slot in range(slots):
        for c in range(2):
            out_ref[slot, c * PAIRS * count : (c + 1) * PAIRS * count, :] = slot_rows(
                z_ref, slot, c, span, count
            )


def order_late(part, sizes, late, perm):
    peers = late.shape[0]
    inputs = perm.shape[1]
    span = PREP * PER_SLOT
    rows = 2 * sizes[1] * span
    depth = 2 * sizes[1] * PER_SLOT
    return pl.pallas_call(
        functools.partial(order_kernel, sizes),
        out_shape=jax.ShapeDtypeStruct((part, depth, inputs), jnp.bfloat16),
        grid=(part // PREP,),
        in_specs=[
            pl.BlockSpec((peers, span, 128), lambda i: (0, i, 0)),
            pl.BlockSpec(perm.shape, lambda i: (0, 0)),
        ],
        out_specs=pl.BlockSpec((PREP, depth, inputs), lambda i: (i, 0, 0)),
        scratch_shapes=[
            pltpu.VMEM((rows, inputs), jnp.bfloat16),
            pltpu.VMEM((inputs // 128, rows + PREP * PER_SLOT, 128), jnp.float32),
        ],
        cost_estimate=pl.CostEstimate(flops=8 * 10**9, bytes_accessed=4 << 20, transcendentals=0),
        compiler_params=pltpu.CompilerParams(
            dimension_semantics=("arbitrary",), vmem_limit_bytes=VMEM
        ),
        name="order_late",
    )(late, perm)


def correlate_kernel(scale, sizes, start, *refs):
    late_ref, arrived_ref, perm_ref = refs[:3]
    out_ref, lhs_ref, z_ref, ordered_ref, buffer_ref, sems = refs[-6:]
    inputs = perm_ref.shape[1]
    span = PREP * PER_SLOT
    count = 2 * sizes[1]
    depth = PAIRS * count
    batches, batch = buffer_ref.shape[:2]
    tile = 128
    tall = lax.broadcasted_iota(jnp.int32, (tile, tile), 0)
    wide = lax.broadcasted_iota(jnp.int32, (tile, tile), 1)
    upper = tall <= wide

    def leave(group, k):
        first = start + group * PREP + k * batch
        return pltpu.make_async_copy(
            buffer_ref.at[k], out_ref.at[pl.ds(first, batch)], sems.at[k]
        )

    def products(z, turned, left, into):
        for at in range(0, inputs, tile):
            rows = slice(at, at + tile)
            sides = jnp.concatenate([turned[:, : at + tile], z[:, at:]], axis=1)
            both = jnp.dot(left[rows], sides, preferred_element_type=jnp.float32) * scale
            if at > 0:
                into[rows, :at] = both[:, :at]
            into[rows, rows] = jnp.where(
                upper, both[:, at + tile : at + 2 * tile], both[:, at : at + tile]
            )
            if at + tile < inputs:
                into[rows, at + tile :] = both[:, at + 2 * tile :]

    def order(group, parity):
        source = arrived_ref.at[:, pl.ds(pl.multiple_of(group * span, span), span), :]
        order_inputs(source, perm_ref, lhs_ref, z_ref, sizes, span)
        for slot in range(PREP):
            for c in range(2):
                ordered_ref[parity, slot, c * depth : (c + 1) * depth, :] = slot_rows(
                    z_ref, slot, c, span, count
                )

    groups = late_ref.shape[0] // PREP

    def work(group, parity, fresh, following):
        for k in range(batches):
            if not fresh:
                leave(group - 1, k).wait()
            if k == 1 and following is not None:
                order(following, 1 - parity)
            for i in range(batch):
                slot = k * batch + i
                z = jnp.concatenate([ordered_ref[parity, slot], late_ref[group * PREP + slot]], axis=0)
                turned = []
                for at in range(0, z.shape[0], 2 * depth):
                    turned += [-z[at + depth : at + 2 * depth], z[at : at + depth]]
                turned = jnp.concatenate(turned, axis=0)
                products(z, turned, z.T, buffer_ref.at[k, i])
            leave(group, k).start()

    order(0, 0)
    if groups <= UNROLLED:
        for group in range(groups):
            work(group, group % 2, group == 0, group + 1 if group + 1 < groups else None)
    else:

        def follow(group, carry):
            work(group, lax.rem(group, 2), False, jnp.minimum(group + 1, groups - 1))
            return carry

        work(0, 0, True, 1)
        lax.fori_loop(1, groups, follow, 0)
    for k in range(batches):
        leave(groups - 1, k).wait()


def correlate(start, part, share, inputs, scale, sizes, late, arrived, perm, before):
    depth = late.shape[1]
    rows = 2 * sizes[1] * PREP * PER_SLOT
    operands = [late, arrived, perm]
    in_specs = [
        pl.BlockSpec((pl.Element(part), pl.Element(depth), pl.Element(inputs)), lambda i: (start, 0, 0)),
        pl.BlockSpec(arrived.shape, lambda i: (0, 0, 0)),
        pl.BlockSpec(perm.shape, lambda i: (0, 0)),
    ]
    aliases = {}
    if before is not None:
        in_specs.append(pl.BlockSpec(memory_space=pl.ANY))
        aliases = {len(operands): 0}
        operands.append(before)
    return pl.pallas_call(
        functools.partial(correlate_kernel, scale, sizes, start),
        out_shape=jax.ShapeDtypeStruct((share, inputs, inputs), jnp.float32),
        grid=(1,),
        in_specs=in_specs,
        out_specs=pl.BlockSpec(memory_space=pl.ANY),
        scratch_shapes=[
            pltpu.VMEM((rows, inputs), jnp.bfloat16),
            pltpu.VMEM((inputs // 128, rows + PREP * PER_SLOT, 128), jnp.float32),
            pltpu.VMEM((2, PREP, depth, inputs), jnp.bfloat16),
            pltpu.VMEM((PREP // BATCHED, BATCHED, inputs, inputs), jnp.float32),
            pltpu.SemaphoreType.DMA((PREP // BATCHED,)),
        ],
        input_output_aliases=aliases,
        cost_estimate=pl.CostEstimate(
            flops=part * 12 * 10**7, bytes_accessed=part * inputs * inputs * 4, transcendentals=0
        ),
        compiler_params=pltpu.CompilerParams(
            dimension_semantics=("arbitrary",), vmem_limit_bytes=VMEM
        ),
        name="correlate",
    )(*operands)


def fused_body(samples, history, station_order, channel_order, flagged):
    row_count, local_length = samples.shape
    spec_local = local_length // NFFT
    st_count = lax.axis_size("st")
    tm_count = lax.axis_size("tm")
    pol_count = lax.axis_size("pol")
    peers = st_count * tm_count * pol_count
    share = CH // peers
    inputs = row_count * st_count
    pol = lax.axis_index("pol")

    ending = lax.dynamic_slice(
        samples, (pol * ROWS, local_length - LEAD * NFFT), (ROWS, LEAD * NFFT)
    )
    halo = lax.ppermute(ending, "tm", [(i, i + 1) for i in range(tm_count - 1)])

    e, f = channel_order % FRAME_A, channel_order // FRAME_A
    row = jnp.minimum(e, FRAME_A - e) * (2 * LOW) + jnp.where(e > HALF_E, LOW, 0) + f
    rows = jnp.arange(CH + 2)
    here = jnp.where(rows == CH, pol, lax.axis_index("tm"))
    rows = jnp.where(rows < CH, jnp.pad(row * PER_SLOT, (0, 2)), here).astype(jnp.int32)
    cosine, sine = np_twist()
    consts = [jnp.asarray(c) for c in (np_window(), np_first(), cosine, sine, np_second())]

    parts = [5 * (share // 8), 3 * (share // 8)]
    groups = ROWS // GROUP
    late = filterbank(
        late_kernel, "filterbank_late", peers, [share], rows, [samples],
        [
            pl.BlockSpec(
                (pl.Element(GROUP), pl.Element((BATCH + LEAD) * NFFT)),
                lambda i, r: ((r[CH] * groups + i) * GROUP, local_length - (BATCH + LEAD) * NFFT),
            )
        ],
        consts,
    )
    exchange = functools.partial(lax.all_to_all, axis_name=AXES, split_axis=0, concat_axis=0, tiled=True)
    late = exchange(late[0])
    early = filterbank(
        early_kernel, "filterbank_early", peers, parts, rows, [samples, halo, history],
        [
            pl.BlockSpec((GROUP, BATCH * NFFT), lambda i, r: (r[CH] * groups + i, 0)),
            pl.BlockSpec((GROUP, LEAD * NFFT), lambda i, r: (jnp.where(r[CH + 1] == 0, 0, i), 0)),
            pl.BlockSpec(
                (GROUP, LEAD * NFFT), lambda i, r: (jnp.where(r[CH + 1] == 0, r[CH] * groups + i, 0), 0)
            ),
        ],
        consts,
    )
    line = jnp.arange(inputs)
    target = 2 * jnp.repeat(station_order, 2) + line % 2
    keep = 1 - jnp.repeat(flagged, 2)
    perm = ((target[:, None] == line[None, :]) & (keep[None, :] == 1)).astype(jnp.bfloat16)

    early, rest, perm = lax.optimization_barrier((*early, perm))
    sizes = (st_count, tm_count, pol_count)
    early = exchange(early)
    late = order_late(share, sizes, late, perm)
    rest, late = lax.optimization_barrier((rest, late))
    rest = exchange(rest)

    scale = 1.0 / (spec_local * tm_count)
    common = (share, inputs, scale, sizes, late)
    out = correlate(0, parts[0], *common, early, perm, None)
    return correlate(parts[0], parts[1], *common, rest, perm, out)


def shifted(array, axis, by):
    peers = lax.axis_size(axis)
    pairs = [(i, i + by) for i in range(peers) if 0 <= i + by < peers]
    return lax.ppermute(array, axis, pairs)


def filter_window(tap_count, frame_size):
    length = tap_count * frame_size
    offsets = jnp.arange(length).astype(jnp.float32) + 0.5
    centred = (offsets - 0.5 * length) / frame_size
    tapering = 0.5 - 0.5 * jnp.cos(offsets * (2.0 * math.pi / length))
    return (jnp.sinc(centred) * tapering).reshape(tap_count, frame_size)


def polyphase(row_block, weights, spec_count):
    row_total = row_block.shape[0]
    tap_count, frame_size = weights.shape
    running = jnp.zeros((row_total, spec_count, frame_size), jnp.float32)
    for tap_index in range(tap_count):
        section = row_block[:, tap_index * frame_size : (tap_index + spec_count) * frame_size]
        section = section.reshape(row_total, spec_count, frame_size)
        running = running + section.astype(jnp.float32) * weights[tap_index]
    return running.astype(jnp.bfloat16).reshape(row_total * spec_count, frame_size)


def trig_pair(left, right, modulus, amplitude):
    turn_count = left[:, None] * right[None, :] % modulus
    angles = turn_count.astype(jnp.float32) * (2.0 * math.pi / modulus)
    cosine = (jnp.cos(angles) * amplitude).astype(jnp.bfloat16)
    sine_part = (-(jnp.sin(angles) * amplitude)).astype(jnp.bfloat16)
    return (cosine, sine_part)


def product_low(form, left, right):
    return jnp.einsum(form, left, right, preferred_element_type=jnp.float32)


def frame_transform(filtered, channels, first_len):
    row_total, frame_size = filtered.shape
    second_len = frame_size // first_len
    half_len = second_len // 2
    first_idx = jnp.arange(first_len)
    second_idx = jnp.arange(second_len)
    half_idx = jnp.arange(half_len)
    first_cos, first_sin = trig_pair(first_idx, first_idx, first_len, 1.0 / math.sqrt(first_len))
    blocks = filtered.reshape(row_total, first_len, second_len)
    segment_re = product_low("rab,ae->reb", blocks, first_cos)
    segment_im = product_low("rab,ae->reb", blocks, first_sin)
    twist_turns = first_idx[:, None] * second_idx[None, :] % frame_size
    twist_angles = twist_turns.astype(jnp.float32) * (2.0 * math.pi / frame_size)
    twist_cos = jnp.cos(twist_angles)
    twist_sin = jnp.sin(twist_angles)
    twist_re = (segment_re * twist_cos + segment_im * twist_sin).astype(jnp.bfloat16)
    twist_im = (segment_im * twist_cos - segment_re * twist_sin).astype(jnp.bfloat16)
    second_cos, second_sin = trig_pair(
        second_idx, half_idx, second_len, 1.0 / math.sqrt(second_len)
    )
    full_re = product_low("reb,bf->ref", twist_re, second_cos) - product_low(
        "reb,bf->ref", twist_im, second_sin
    )
    full_im = product_low("reb,bf->ref", twist_re, second_sin) + product_low(
        "reb,bf->ref", twist_im, second_cos
    )
    column = channels % first_len * half_len + channels // first_len
    flat_re = jnp.take(full_re.reshape(row_total, first_len * half_len), column, axis=1)
    flat_im = jnp.take(full_im.reshape(row_total, first_len * half_len), column, axis=1)
    return jnp.stack([flat_re, flat_im], axis=1)


def input_rows(station_order):
    station_total = station_order.shape[0]
    inverse = (
        jnp.zeros((station_total,), jnp.int32).at[station_order].set(jnp.arange(station_total))
    )
    polarity = jnp.tile(jnp.arange(2), station_total)
    return 2 * jnp.repeat(inverse, 2) + polarity


def packed_products(turned, norm_scale):
    input_count, spec_count, pair_count, slot_count = turned.shape
    arranged = turned.transpose(3, 0, 1, 2)
    stacked = arranged.reshape(slot_count, input_count, spec_count * 2)
    swapped = jnp.stack([-arranged[..., 1], arranged[..., 0]], axis=-1).reshape(
        slot_count, input_count, spec_count * 2
    )
    combined = jnp.concatenate([stacked, swapped], axis=1)
    visible = jnp.einsum("sik,sjk->sij", stacked, combined, preferred_element_type=jnp.float32)
    indices = jnp.arange(input_count)
    upper_half = indices[:, None] <= indices[None, :]
    return (
        jnp.where(upper_half[None], visible[:, :, :input_count], visible[:, :, input_count:])
        * norm_scale
    )


def general_body(samples, history, station_order, channel_order, flagged):
    row_count, local_length = samples.shape
    spec_local = local_length // NFFT
    st_count = lax.axis_size("st")
    tm_count = lax.axis_size("tm")
    pol_count = lax.axis_size("pol")
    slot_share = CH // (st_count * tm_count * pol_count)
    half_slots = CH // pol_count
    lead_length = (TAPS - 1) * NFFT
    earlier = shifted(samples[:, local_length - lead_length :], "tm", 1)
    earlier = jnp.where(lax.axis_index("tm") == 0, history, earlier)
    stream = jnp.concatenate([earlier, samples], axis=1)
    filtered = polyphase(stream, filter_window(TAPS, NFFT), spec_local)
    local_slots = jnp.arange(half_slots)
    global_slots = (
        local_slots // slot_share * (slot_share * pol_count)
        + lax.axis_index("pol") * slot_share
        + local_slots % slot_share
    )
    station_ids = lax.dynamic_slice_in_dim(
        station_order, lax.axis_index("st") * (row_count // 2), row_count // 2
    )
    keeping = jnp.repeat((1 - flagged[station_ids]).astype(jnp.float32), 2)
    product = frame_transform(filtered, channel_order[global_slots], FRAME_A)
    product = product.reshape(row_count, spec_local, 2, half_slots) * keeping[:, None, None, None]
    spectra = product.astype(jnp.bfloat16)
    norm_scale = 1.0 / (spec_local * tm_count)
    input_order = input_rows(station_order)
    turned = lax.all_to_all(
        lax.all_to_all(spectra, "st", split_axis=3, concat_axis=0, tiled=True),
        "tm",
        split_axis=3,
        concat_axis=1,
        tiled=True,
    )
    turned = jnp.take(turned, input_order, axis=0)
    return packed_products(turned, norm_scale)


def fits(samples, mesh):
    st_count, tm_count, pol_count = (mesh.shape[a] for a in AXES)
    rows = samples.shape[0] // st_count
    frames = samples.shape[1] // tm_count // NFFT
    share = CH // (st_count * tm_count * pol_count)
    return (
        rows == ROWS * pol_count
        and frames == 2 * BATCH
        and tm_count == 4
        and pol_count == 2
        and share % (8 * PREP) == 0
        and samples.shape[0] % 256 == 0
    )


def solution(mesh):
    def run(samples, history, station_order, channel_order, flagged):
        body = fused_body if fits(samples, mesh) else general_body
        return jax.shard_map(
            body,
            mesh=mesh,
            in_specs=(P("st", "tm"), P("st", None), P(), P(), P()),
            out_specs=P(("st", "tm", "pol"), None, None),
            check_vma=False,
        )(samples, history, station_order, channel_order, flagged)

    return run
```
